256 devices in a mesh: wide: 32 (over y_lo, z, core), narrow: 8 (over x, y_hi).
Axes of the slice: x: 4, y: 4 (y_hi: 2, y_lo: 2; y = y_hi * 2 + y_lo), z: 8, core: 2. Of those that a mesh axis runs over, the one named last changes fastest.
Arguments:
- pair: bfloat16 [768, 768, 128], P('wide', 'narrow'), may hold values from -6 to 6
- tile_mask: int32 [6, 6], replicated, may hold values 0 or 1
- chain_ids: int32 [768], replicated, may hold values from 0 to 3, never falling along the last dimension, each value on 1 to 384 neighbouring positions
- in_gain: float32 [128], replicated, may hold values from 0.1 to 1.9
- in_bias: float32 [128], replicated, may hold values from -3 to 3
- w_ab: bfloat16 [128, 512], replicated, may hold values from -0.5 to 0.5
- w_gate: bfloat16 [128, 128], replicated, may hold values from -0.5 to 0.5
- out_gain: float32 [128], replicated, may hold values from 0.1 to 1.9
- out_bias: float32 [128], replicated, may hold values from -3 to 3
- w_out: bfloat16 [128, 128], replicated, may hold values from -0.5 to 0.5
Outputs:
- update: bfloat16 [768, 768, 128], P('wide', 'narrow')
The draws below stay inside these ranges and needn't reach their ends.
Inputs may be any that keep to these rules, and one draw needn't show every extreme that they name: `chain_ids`: chain numbers never fall along the tokens.
All inputs are finite; a program needn't handle non-finite values.
Results may differ from the reference program's by a relative error of at most 0.0062.
Values may be sent and summed in bfloat16 or wider, within the bound.
A program may use at most 128 MiB of HBM per device.

```python
import math
import jax
import jax.numpy as jnp
import numpy as np
from jax import lax

C = 128
HID = 128
TILE = 128
CHAINS = 4
N = 768
NT = 6


def place_ends(values, rng, smallest, largest):
    extent = values.shape
    spot = [jax.random.randint(jax.random.fold_in(rng, axis), (), 0, extent[axis]) for axis in range(len(extent))]
    values = values.at[tuple(spot)].set(smallest)
    longest = extent.index(max(extent))
    spot[longest] = (spot[longest] + 1) % extent[longest]
    return values.at[tuple(spot)].set(largest)


def block_levels(rng, dims, pieces, least, high):
    factor_of, own = 1.0, jax.random.fold_in(rng, 6)
    for axis_at, parts in pieces:
        steps = jnp.exp(jax.random.uniform(jax.random.fold_in(own, axis_at), (parts,), jnp.float32, least / len(pieces), high / len(pieces)))
        factor_of = factor_of * jnp.repeat(steps, dims[axis_at] // parts).reshape([-1 if axis == axis_at else 1 for axis in range(len(dims))])
    return factor_of


def length_profile(amount, total, most, slope):
    loads = [(1 << 20) // math.isqrt(standing ** slope) + 1 for standing in range(2, amount + 1)]
    surplus, counts = total - most - (amount - 1), [1] * (amount - 1)
    while surplus > 0:
        free = [i for i in range(amount - 1) if counts[i] < most]
        mass, left = sum([loads[i] for i in free]), surplus
        for i in free:
            more = min(most - counts[i], max(1, left * loads[i] // mass), surplus)
            counts[i] = counts[i] + more
            surplus = surplus - more
    return np.array([most] + counts)


def ragged_sizes(key, count, total, most, lean):
    if count == 2:
        one = jax.random.randint(key, (), max(1, total - most), min(most, total - 1) + 1)
        return jnp.stack([one, total - one])
    tallies = jnp.asarray(length_profile(count, total, most, lean), jnp.int32)
    pairs = (count - 1) // 2
    donor, taker = tallies[1:1 + 2 * pairs:2], tallies[2:2 + 2 * pairs:2]
    margin = jnp.minimum(donor - 1, most - taker)
    moved = jax.random.randint(jax.random.fold_in(key, 1), (pairs,), 0, 1 << 20) % (margin + 1)
    tallies = tallies.at[1:1 + 2 * pairs:2].set(donor - moved).at[2:2 + 2 * pairs:2].set(taker + moved)
    return tallies[jax.random.permutation(jax.random.fold_in(key, 2), count)]


def normal_values(stream_key, extent, deviation, bound, shards=(), held_as=jnp.bfloat16):
    drawn = jax.random.normal(stream_key, extent, jnp.float32) * deviation
    if len(shards) > 0:
        drawn = block_levels(stream_key, extent, shards, -0.22, 0.18) * drawn
    return jnp.clip(drawn, min=-bound, max=bound).astype(held_as)


def setup_inputs(seed: int = 0) -> dict:
    streams_of = jax.random.split(jax.random.key(seed), 11)
    pair = normal_values(streams_of[0], (N, N, C), 1.0, 6.0, ((0, 32), (1, 8)))
    tile_mask = place_ends((jax.random.randint(streams_of[1], (NT, NT), 0, 2) < 1).astype(jnp.int32), jax.random.fold_in(streams_of[1], 1), 0, 1)
    chain_ids = jnp.searchsorted(jnp.cumsum(ragged_sizes(streams_of[2], CHAINS, N, N // 2, 0)), jnp.arange(N), side="right").astype(jnp.int32)
    in_gain = jnp.clip(1.0 + 0.18 * jax.random.normal(streams_of[3], (C,), jnp.float32), 0.1, 1.9)
    in_bias = normal_values(streams_of[4], (C,), 0.5, 3.0, (), jnp.float32)
    w_ab = normal_values(streams_of[5], (C, 4 * HID), C ** -0.5, 0.5)
    w_gate = normal_values(streams_of[6], (C, C), C ** -0.5, 0.5)
    out_gain = jnp.clip(1.0 + 0.18 * jax.random.normal(streams_of[7], (HID,), jnp.float32), 0.1, 1.9)
    out_bias = normal_values(streams_of[8], (HID,), 0.5, 3.0, (), jnp.float32)
    w_out = normal_values(streams_of[9], (HID, C), HID ** -0.5, 0.5)
    return {"pair": pair, "tile_mask": tile_mask, "chain_ids": chain_ids, "in_gain": in_gain, "in_bias": in_bias, "w_ab": w_ab, "w_gate": w_gate, "out_gain": out_gain, "out_bias": out_bias, "w_out": w_out}


def normalize(values, gain, bias, axis):
    mean = lax.optimization_barrier(jnp.mean(values, axis=axis, keepdims=True))
    centred = values - mean
    spread = lax.optimization_barrier(jnp.mean(centred * centred, axis=axis, keepdims=True))
    return centred * lax.rsqrt(spread + 1e-05) * gain + bias

def pair_mask(tile_mask, chain_ids, row_start, rows, col_start, cols):
    count = tile_mask.shape[0]
    tiles = jnp.arange(count, dtype=jnp.int32)
    row_index = row_start + jnp.arange(rows, dtype=jnp.int32)
    col_index = col_start + jnp.arange(cols, dtype=jnp.int32)
    row_onehot = (row_index[:, None] // TILE == tiles[None, :]).astype(jnp.float32)
    col_onehot = (col_index[:, None] // TILE == tiles[None, :]).astype(jnp.float32)
    blocked = jnp.dot(jnp.dot(row_onehot, tile_mask.astype(jnp.float32), precision=lax.Precision.HIGHEST), col_onehot.T, precision=lax.Precision.HIGHEST)
    row_chain = lax.dynamic_slice_in_dim(chain_ids, row_start, rows)
    col_chain = lax.dynamic_slice_in_dim(chain_ids, col_start, cols)
    same = (row_chain[:, None] == col_chain[None, :]).astype(jnp.float32)
    return jnp.maximum(blocked, same)

def gated_pair(normed, weights, mask, width):
    proj = jnp.einsum('rkc,cd->drk', normed.astype(jnp.float32), weights.astype(jnp.float32))
    left_side = mask * jax.nn.sigmoid(proj[:width]) * proj[width:2 * width]
    right_side = mask * jax.nn.sigmoid(proj[2 * width:3 * width]) * proj[3 * width:]
    return jnp.stack([left_side, right_side]).astype(jnp.bfloat16)

def reference(pair, tile_mask, chain_ids, in_gain, in_bias, w_ab, w_gate, out_gain, out_bias, w_out):
    normed = normalize(pair.astype(jnp.float32), in_gain, in_bias, 2).astype(jnp.bfloat16)
    mask = pair_mask(tile_mask, chain_ids, 0, N, 0, N)

    def block_sides(inputs):
        rows_normed, rows_mask = inputs
        return gated_pair(rows_normed, w_ab, rows_mask, HID)
    blocks = lax.map(block_sides, (normed.reshape(NT, TILE, N, C), mask.reshape(NT, TILE, N)))
    sides = jnp.transpose(blocks, (1, 2, 0, 3, 4)).reshape(2, HID, N, N)
    product = jnp.einsum('cik,cjk->cij', sides[0].astype(jnp.float32), sides[1].astype(jnp.float32)).astype(jnp.bfloat16)
    product_normed = normalize(product.astype(jnp.float32), out_gain[:, None, None], out_bias[:, None, None], 0).astype(jnp.bfloat16)
    projected = jnp.einsum('hij,hc->ijc', product_normed.astype(jnp.float32), w_out.astype(jnp.float32))
    gate = jax.nn.sigmoid(jnp.einsum('ijc,cd->ijd', normed.astype(jnp.float32), w_gate.astype(jnp.float32)))
    return (gate * projected).astype(jnp.bfloat16)
```

```python
import functools

import jax
import jax.numpy as jnp
from jax import lax
from jax.experimental import pallas as pl
from jax.experimental.pallas import tpu as pltpu
from jax.sharding import PartitionSpec as P

MESH = pl.DeviceIdType.MESH
F32, BF16 = jnp.float32, jnp.bfloat16
CHIPS = 128
ROWS, COLS, C = 24, 96, 128
MSG = 40
TILES = 24
EPS = 1e-05


def sigmoid(x):
    return 0.5 * jnp.tanh(0.5 * x) + 0.5


def dot(a, b, ca, cb):
    return lax.dot_general(a, b, (((ca,), (cb,)), ((), ())), preferred_element_type=F32)


def keep_mask(wide, narrow, tile_ref, chain_ref):
    tile = lax.broadcasted_iota(jnp.int32, (TILES, 128), 0)
    lane = lax.broadcasted_iota(jnp.int32, (TILES, 128), 1)
    body, main = tile < 16, lane < 96
    i = jnp.where(body & jnp.logical_not(main), 16 + tile % 8, tile)
    k = jnp.where(body, jnp.where(main, lane, lane - 96 + 32 * (tile // 8)), 64 + lane % 32)
    i = i + wide * ROWS
    k = k + narrow * COLS
    chain_i = jnp.zeros((TILES, 128), jnp.int32)
    chain_k = jnp.zeros((TILES, 128), jnp.int32)
    chains = chain_ref[...]
    for q in range(1, 4):
        below = (chains < q).astype(F32)
        start = jnp.sum(jnp.sum(below, axis=0, keepdims=True), axis=1, keepdims=True).astype(jnp.int32)
        chain_i = chain_i + (i >= start).astype(jnp.int32)
        chain_k = chain_k + (k >= start).astype(jnp.int32)
    same = (chain_i == chain_k).astype(F32)
    row_tile, col_tile = i // 128, k // 128
    blocked = jnp.zeros((TILES, 128), F32)
    for a in range(6):
        in_row = row_tile == a
        for b in range(6):
            value = tile_ref[a, b].astype(F32)
            blocked = blocked + jnp.where(in_row & (col_tile == b), value, 0.0)
    return jnp.maximum(blocked, same)


def kernel(
    pair_ref, tile_ref, chain_ref, in_gain_ref, in_bias_ref, w_ab_ref, w_gate_ref, out_gain_ref, out_bias_ref, w_out_ref,
    out_ref,
    normed_ref, packed_ref, mask_ref, w_t_ref, stage_ref, send_ref, recv_ref, gate_ref, a_ref, b_ref, back_ref, home_ref,
    sums_ref, s_send, s_recv, s_swap_send, s_swap_recv, s_back, s_home,
):
    wide, narrow = lax.axis_index("wide"), lax.axis_index("narrow")
    w16, core = wide // 2, wide % 2
    y_lo, z = wide // 16, (wide // 2) % 8
    x, y = narrow // 2, (narrow % 2) * 2 + y_lo
    me = w16 * 8 + narrow

    def peer(d):
        pz = (z + d % 8) % 8
        py = (y + (d // 8) % 4) % 4
        px = (x + d // 32) % 4
        p16 = (py % 2) * 8 + pz
        pn = px * 2 + py // 2
        return p16 * 8 + pn, (p16 * 2 + core, pn)

    sibling = (w16 * 2 + 1 - core, narrow)
    barrier = pltpu.get_barrier_semaphore()
    pl.semaphore_signal(barrier, inc=1, device_id=sibling, device_id_type=MESH)

    def greet(d, _):
        pl.semaphore_signal(barrier, inc=1, device_id=peer(d)[1], device_id_type=MESH)
        return 0

    lax.fori_loop(1, CHIPS, greet, 0)

    w_t_ref[...] = w_ab_ref[...].T
    mask_ref[...] = keep_mask(wide, narrow, tile_ref, chain_ref)

    def norm_row(i):
        values = pair_ref[i].astype(F32)
        mean = jnp.mean(values, axis=1, keepdims=True)
        centred = values - mean
        spread = jnp.mean(centred * centred, axis=1, keepdims=True)
        normed = (centred * lax.rsqrt(spread + EPS) * in_gain_ref[...] + in_bias_ref[...]).astype(BF16)
        normed_ref[i] = normed
        return normed

    def norm_body(i, _):
        packed_ref[i, 0:96] = norm_row(i)
        return 0

    def norm_tail(r, _):
        normed = norm_row(16 + r)
        packed_ref[r, 96:128] = normed[0:32]
        packed_ref[8 + r, 96:128] = normed[32:64]
        last = normed[64:96]
        for q in range(4):
            packed_ref[16 + r, 32 * q : 32 * q + 32] = last
        return 0

    lax.fori_loop(0, 16, norm_body, 0)
    lax.fori_loop(0, 8, norm_tail, 0)

    def sides(t):
        proj = dot(w_t_ref[...], packed_ref[t], 1, 1)
        mask = mask_ref[pl.ds(t, 1), :]
        left = mask * sigmoid(proj[0:128]) * proj[128:256]
        right = mask * sigmoid(proj[256:384]) * proj[384:512]
        return left, right

    def project(t, _):
        left, right = sides(t)
        stage_ref[pl.ds(t, CHIPS, stride=MSG), :] = left
        stage_ref[pl.ds(16 + t, CHIPS, stride=MSG), :] = right
        return 0

    lane8 = lax.broadcasted_iota(jnp.int32, (8, 128), 1)

    def project_tail(t, _):
        left, right = sides(t)
        lane = lax.broadcasted_iota(jnp.int32, (128, 128), 1)
        stage_ref[pl.ds(16 + t, CHIPS, stride=MSG), :] = jnp.where(lane < 32, left, right)
        return 0

    lax.fori_loop(0, 16, project, 0)
    lax.fori_loop(16, 24, project_tail, 0)

    def cast(c, _):
        start = pl.multiple_of(c * MSG, 8)
        send_ref[c] = stage_ref[pl.ds(start, MSG), :].astype(BF16)
        return 0

    lax.fori_loop(0, CHIPS, cast, 0, unroll=4)

    pl.semaphore_wait(barrier, CHIPS)

    def send(d, _):
        chip, device = peer(d)
        pltpu.make_async_remote_copy(
            src_ref=send_ref.at[chip], dst_ref=recv_ref.at[me], send_sem=s_send, recv_sem=s_recv,
            device_id=device, device_id_type=MESH,
        ).start()
        return 0

    lax.fori_loop(1, CHIPS, send, 0)
    recv_ref[me] = send_ref[me]

    def gates(i, _):
        gate_ref[i] = sigmoid(dot(normed_ref[i], w_gate_ref[...], 1, 0))
        return 0

    lax.fori_loop(0, ROWS, gates, 0)
    for p in range(8):
        b_ref[p, 96:128] = jnp.zeros((32, 1024), BF16)

    others = pl.ds(0, CHIPS - 1)
    pltpu.make_async_copy(recv_ref.at[others], recv_ref.at[others], s_recv).wait()
    pltpu.make_async_copy(send_ref.at[others], send_ref.at[others], s_send).wait()

    def unpack(slot):
        f = recv_ref[slot].astype(F32)
        lane = lane8
        low = f[32:40]
        zero = jnp.zeros((8, 128), F32)

        def rest(top, middle, shift):
            return jnp.where(
                lane < 32, pltpu.roll(top, 32, 1),
                jnp.where(lane < 64, pltpu.roll(middle, 64, 1), jnp.where(lane < 96, pltpu.roll(low, shift, 1), zero)),
            )

        left = [jnp.where(lane < 96, f[0:8], zero), jnp.where(lane < 96, f[8:16], zero), rest(f[0:8], f[8:16], 64)]
        right = [f[16:24], f[24:32], rest(f[16:24], f[24:32], 32)]
        return left, right

    def assemble(p, _):
        for n in range(8):
            left0, right0 = unpack(p * 16 + n)
            left1, right1 = unpack(p * 16 + 8 + n)
            columns = slice(128 * n, 128 * n + 128)
            a_ref[pl.ds(pl.multiple_of(p * 48, 16), 48), columns] = jnp.concatenate(left0 + left1, axis=0).astype(BF16)
            b_ref[p, pl.ds(pl.multiple_of(core * 48, 16), 48), columns] = jnp.concatenate(right0 + right1, axis=0).astype(BF16)
        return 0

    lax.fori_loop(0, 8, assemble, 0)

    half = b_ref.at[:, pl.ds(pl.multiple_of(core * 48, 16), 48), :]
    swap = pltpu.make_async_remote_copy(
        src_ref=half, dst_ref=half, send_sem=s_swap_send, recv_sem=s_swap_recv, device_id=sibling, device_id_type=MESH
    )
    swap.start()
    swap.wait()

    def multiply(p, _):
        product = dot(a_ref[...], b_ref[p], 1, 1)
        for w in range(16):
            back_ref[w * 8 + p] = product[24 * w : 24 * w + 24].astype(BF16)
        return 0

    lax.fori_loop(0, 8, multiply, 0)

    def send_back(d, _):
        chip, device = peer(d)
        pltpu.make_async_remote_copy(
            src_ref=back_ref.at[chip], dst_ref=home_ref.at[me], send_sem=s_back, recv_sem=s_home,
            device_id=device, device_id_type=MESH,
        ).start()
        return 0

    lax.fori_loop(1, CHIPS, send_back, 0)
    home_ref[me] = back_ref[me]
    pltpu.make_async_copy(home_ref.at[others], home_ref.at[others], s_home).wait()
    pltpu.make_async_copy(back_ref.at[others], back_ref.at[others], s_back).wait()

    def widen(c, _):
        sums_ref[pl.ds(pl.multiple_of(c * ROWS, 8), ROWS), :] = home_ref[c].astype(F32)
        return 0

    lax.fori_loop(0, CHIPS, widen, 0, unroll=4)

    def finish(i, _):
        values = sums_ref[pl.ds(i, CHIPS, stride=ROWS), :]
        mean = jnp.mean(values, axis=0, keepdims=True)
        centred = values - mean
        spread = jnp.mean(centred * centred, axis=0, keepdims=True)
        normed = (centred * lax.rsqrt(spread + EPS) * out_gain_ref[...] + out_bias_ref[...]).astype(BF16)
        projected = dot(normed, w_out_ref[...], 0, 0)
        natural = jnp.concatenate([projected[0:24], projected[48:72], projected[24:48], projected[72:96]], axis=0)
        out_ref[i] = (gate_ref[i] * natural).astype(BF16)
        return 0

    lax.fori_loop(0, ROWS, finish, 0)


def shards(pair, tile_mask, chain_ids, in_gain, in_bias, w_ab, w_gate, out_gain, out_bias, w_out):
    vmem = pl.BlockSpec(memory_space=pltpu.VMEM)
    smem = pl.BlockSpec(memory_space=pltpu.SMEM)
    return pl.pallas_call(
        kernel,
        out_shape=jax.ShapeDtypeStruct((ROWS, COLS, C), BF16),
        in_specs=[vmem, smem] + [vmem] * 8,
        out_specs=vmem,
        scratch_shapes=[
            pltpu.VMEM((ROWS, COLS, C), BF16),
            pltpu.VMEM((TILES, 128, C), BF16),
            pltpu.VMEM((TILES, 128), F32),
            pltpu.VMEM((512, C), BF16),
            pltpu.VMEM((CHIPS * MSG, 128), F32),
            pltpu.VMEM((CHIPS, MSG, 128), BF16),
            pltpu.VMEM((CHIPS, MSG, 128), BF16),
            pltpu.VMEM((ROWS, COLS, C), F32),
            pltpu.VMEM((384, 1024), BF16),
            pltpu.VMEM((8, 128, 1024), BF16),
            pltpu.VMEM((CHIPS, ROWS, 128), BF16),
            pltpu.VMEM((CHIPS, ROWS, 128), BF16),
            pltpu.VMEM((CHIPS * ROWS, 128), F32),
        ]
        + [pltpu.SemaphoreType.DMA(())] * 6,
        compiler_params=pltpu.CompilerParams(collective_id=1, has_side_effects=True, vmem_limit_bytes=48 << 20),
    )(
        pair, tile_mask, chain_ids.reshape(6, 128), in_gain.reshape(1, C), in_bias.reshape(1, C), w_ab, w_gate,
        jnp.broadcast_to(out_gain[:, None], (C, 128)), jnp.broadcast_to(out_bias[:, None], (C, 128)), w_out,
    )


def solution(mesh):
    in_specs = (P("wide", "narrow", None), P(), P(), P(), P(), P(), P(), P(), P(), P())
    out_specs = P("wide", "narrow", None)
    return jax.shard_map(shards, mesh=mesh, in_specs=in_specs, out_specs=out_specs, check_vma=False)
```

```python
import functools

import jax
import jax.numpy as jnp
from jax import lax
from jax.experimental import pallas as pl
from jax.experimental.pallas import tpu as pltpu
from jax.sharding import PartitionSpec as P

MESH = pl.DeviceIdType.MESH
F32, BF16 = jnp.float32, jnp.bfloat16
CHIPS = 128
ROWS, COLS, C = 24, 96, 128
MSG = 40
TILES = 24
EPS = 1e-05


def sigmoid(x):
    return 0.5 * jnp.tanh(0.5 * x) + 0.5


def dot(a, b, ca, cb):
    return lax.dot_general(a, b, (((ca,), (cb,)), ((), ())), preferred_element_type=F32)


def keep_mask(wide, narrow, tile_ref, chain_ref):
    tile = lax.broadcasted_iota(jnp.int32, (TILES, 128), 0)
    lane = lax.broadcasted_iota(jnp.int32, (TILES, 128), 1)
    body, main = tile < 16, lane < 96
    i = jnp.where(body & jnp.logical_not(main), 16 + tile % 8, tile)
    k = jnp.where(body, jnp.where(main, lane, lane - 96 + 32 * (tile // 8)), 64 + lane % 32)
    i = i + wide * ROWS
    k = k + narrow * COLS
    chain_i = jnp.zeros((TILES, 128), jnp.int32)
    chain_k = jnp.zeros((TILES, 128), jnp.int32)
    chains = chain_ref[...]
    for q in range(1, 4):
        below = (chains < q).astype(F32)
        start = jnp.sum(jnp.sum(below, axis=0, keepdims=True), axis=1, keepdims=True).astype(jnp.int32)
        chain_i = chain_i + (i >= start).astype(jnp.int32)
        chain_k = chain_k + (k >= start).astype(jnp.int32)
    same = (chain_i == chain_k).astype(F32)
    row_tile, col_tile = i // 128, k // 128
    blocked = jnp.zeros((TILES, 128), F32)
    for a in range(6):
        in_row = row_tile == a
        for b in range(6):
            value = tile_ref[a : a + 1, b : b + 1].astype(F32)
            blocked = blocked + jnp.where(in_row & (col_tile == b), value, 0.0)
    return jnp.maximum(blocked, same)


def kernel(
    pair_hbm, tile_hbm, chain_hbm, in_gain_hbm, in_bias_hbm, w_ab_hbm, w_gate_hbm, out_gain_hbm, out_bias_hbm, w_out_hbm,
    out_ref,
    pair_ref, tile_ref, chain_ref, in_gain_ref, in_bias_ref, w_ab_ref, w_gate_ref, out_gain_ref, out_bias_ref, w_out_ref,
    normed_ref, packed_ref, mask_ref, w_t_ref, stage_ref, send_ref, recv_ref, gate_ref, a_ref, b_ref, total_ref, back_ref,
    home_ref, sums_ref, gain_ref, bias_ref,
    s_in, s_line, s_plane, s_send, s_recv, s_swap_send, s_swap_recv, s_back, s_home,
):
    wide, narrow = lax.axis_index("wide"), lax.axis_index("narrow")
    w16, core = wide // 2, wide % 2
    y_lo, z = wide // 16, w16 % 8
    x, y = narrow // 2, (narrow % 2) * 2 + y_lo
    me = x * 32 + y * 8 + z

    def device_at(px, py, pz):
        return ((py % 2) * 16 + pz * 2 + core, px * 2 + py // 2)

    sibling = (w16 * 2 + 1 - core, narrow)
    line_z = [device_at(x, y, (z + d) % 8) for d in range(1, 8)]
    line_y = [device_at(x, (y + d) % 4, z) for d in range(1, 4)]
    line_x = [device_at((x + d) % 4, y, z) for d in range(1, 4)]

    inputs = [
        pltpu.make_async_copy(source, target, s_in.at[at])
        for at, (source, target) in enumerate((
            (pair_hbm, pair_ref), (tile_hbm, tile_ref), (chain_hbm, chain_ref), (in_gain_hbm, in_gain_ref),
            (in_bias_hbm, in_bias_ref), (w_ab_hbm, w_ab_ref), (w_gate_hbm, w_gate_ref), (out_gain_hbm, out_gain_ref),
            (out_bias_hbm, out_bias_ref), (w_out_hbm, w_out_ref),
        ))
    ]
    for copy in inputs:
        copy.start()

    barrier = pltpu.get_barrier_semaphore()
    greeted = [sibling] + line_z + line_y + line_x
    for device in greeted:
        pl.semaphore_signal(barrier, inc=1, device_id=device, device_id_type=MESH)

    for copy in inputs:
        copy.wait()

    w_t_ref[...] = w_ab_ref[...].T
    mask_ref[...] = keep_mask(wide, narrow, tile_ref, chain_ref)
    gain_ref[...] = jnp.broadcast_to(out_gain_ref[...], (C, 128)).T
    bias_ref[...] = jnp.broadcast_to(out_bias_ref[...], (C, 128)).T

    pl.semaphore_wait(barrier, len(greeted))
    for device in line_y:
        pl.semaphore_signal(s_line, inc=1, device_id=device, device_id_type=MESH)

    def norm_row(i):
        values = pair_ref[i].astype(F32)
        mean = jnp.mean(values, axis=1, keepdims=True)
        centred = values - mean
        spread = jnp.mean(centred * centred, axis=1, keepdims=True)
        normed = (centred * lax.rsqrt(spread + EPS) * in_gain_ref[...] + in_bias_ref[...]).astype(BF16)
        normed_ref[i] = normed
        return normed

    def norm_body(i, _):
        packed_ref[i, 0:96] = norm_row(i)
        return 0

    def norm_tail(r, _):
        normed = norm_row(16 + r)
        packed_ref[r, 96:128] = normed[0:32]
        packed_ref[8 + r, 96:128] = normed[32:64]
        last = normed[64:96]
        for q in range(4):
            packed_ref[16 + r, 32 * q : 32 * q + 32] = last
        return 0

    lax.fori_loop(0, 16, norm_body, 0, unroll=2)
    lax.fori_loop(0, 8, norm_tail, 0, unroll=2)

    pl.semaphore_wait(s_line, len(line_y))
    for device in line_x:
        pl.semaphore_signal(s_plane, inc=1, device_id=device, device_id_type=MESH)

    lane32 = lax.broadcasted_iota(jnp.int32, (32, 128), 1)

    def send_chunk(dx):
        px = (x + dx) % 4
        first = pl.multiple_of(px * 32, 32)
        weights = jnp.concatenate([w_t_ref[pl.ds(g * 128 + first, 32), :] for g in range(4)], axis=0)

        def sides(t):
            proj = dot(weights, packed_ref[pl.ds(t, 2)].reshape(256, C), 1, 1)
            result = []
            for q in range(2):
                part = proj[:, 128 * q : 128 * q + 128]
                mask = mask_ref[pl.ds(t + q, 1), :]
                left = mask * sigmoid(part[0:32]) * part[32:64]
                right = mask * sigmoid(part[64:96]) * part[96:128]
                result.append((left, right))
            return result

        def project(h, _):
            t = 2 * h
            for q, (left, right) in enumerate(sides(t)):
                stage_ref[pl.ds(t + q, 32, stride=MSG), :] = left
                stage_ref[pl.ds(16 + t + q, 32, stride=MSG), :] = right
            return 0

        def project_tail(h, _):
            t = 2 * h
            for q, (left, right) in enumerate(sides(t)):
                stage_ref[pl.ds(16 + t + q, 32, stride=MSG), :] = jnp.where(lane32 < 32, left, right)
            return 0

        lax.fori_loop(0, 8, project, 0, unroll=2)
        lax.fori_loop(8, 12, project_tail, 0, unroll=2)

        def cast(c):
            start = pl.multiple_of(c * MSG, 8)
            send_ref[px * 32 + c] = stage_ref[pl.ds(start, MSG), :].astype(BF16)

        def send(d, _):
            py, pz = (y + d // 8) % 4, (z + d % 8) % 8
            slot = px * 32 + py * 8 + pz
            pltpu.make_async_remote_copy(
                src_ref=send_ref.at[slot], dst_ref=recv_ref.at[me], send_sem=s_send, recv_sem=s_recv.at[dx],
                device_id=device_at(px, py, pz), device_id_type=MESH,
            ).start()
            return 0

        def cast_body(c, _):
            cast(c)
            return 0

        lax.fori_loop(0, 32, cast_body, 0, unroll=4)
        if dx == 0:
            pl.semaphore_wait(s_plane, len(line_x))
        lax.fori_loop(1 if dx == 0 else 0, 32, send, 0)
        if dx == 0:
            recv_ref[me] = send_ref[me]

    for dx in range(4):
        send_chunk(dx)

    def gates(i, _):
        gate_ref[i] = sigmoid(dot(normed_ref[i], w_gate_ref[...], 1, 0))
        return 0

    lax.fori_loop(0, ROWS, gates, 0)
    for dx in range(4):
        for p in range(8):
            b_ref[dx, p, 96:128] = jnp.zeros((32, 256), BF16)

    lane = lax.broadcasted_iota(jnp.int32, (8, 128), 1)

    def unpack(slot):
        f = recv_ref[slot].astype(F32)
        low = f[32:40]
        zero = jnp.zeros((8, 128), F32)

        def rest(top, middle, shift):
            return jnp.where(
                lane < 32, pltpu.roll(top, 32, 1),
                jnp.where(lane < 64, pltpu.roll(middle, 64, 1), jnp.where(lane < 96, pltpu.roll(low, shift, 1), zero)),
            )

        left = [jnp.where(lane < 96, f[0:8], zero), jnp.where(lane < 96, f[8:16], zero), rest(f[0:8], f[8:16], 64)]
        right = [f[16:24], f[24:32], rest(f[16:24], f[24:32], 32)]
        return left, right

    mine = pl.ds(pl.multiple_of(core * 48, 16), 48)

    def swap(dx):
        half = b_ref.at[dx, :, mine, :]
        return pltpu.make_async_remote_copy(
            src_ref=half, dst_ref=half, send_sem=s_swap_send.at[dx], recv_sem=s_swap_recv.at[dx], device_id=sibling,
            device_id_type=MESH,
        )

    def receive(dx):
        arrived = recv_ref.at[pl.ds(0, 31 if dx == 0 else 32)]
        pltpu.make_async_copy(arrived, arrived, s_recv.at[dx]).wait()
        first = ((x + 4 - dx) % 4) * 32

        def assemble(p, _):
            for q in range(2):
                left0, right0 = unpack(first + 16 * q + 2 * p)
                left1, right1 = unpack(first + 16 * q + 2 * p + 1)
                columns = slice(128 * q, 128 * q + 128)
                rows = pl.ds(pl.multiple_of(p * 48, 16), 48)
                a_ref[dx, rows, columns] = jnp.concatenate(left0 + left1, axis=0).astype(BF16)
                b_ref[dx, p, mine, columns] = jnp.concatenate(right0 + right1, axis=0).astype(BF16)
            return 0

        lax.fori_loop(0, 8, assemble, 0)
        swap(dx).start()

    def partial(dx, px):
        return dot(a_ref[dx], b_ref[dx, pl.ds(2 * px, 2)].reshape(256, 256), 1, 1)

    def multiply(dx):
        swap(dx).wait()

        def step(px, _):
            if dx == 0:
                total_ref[px] = partial(dx, px)
            else:
                total_ref[px] += partial(dx, px)
            return 0

        lax.fori_loop(0, 4, step, 0)

    for dx in range(4):
        receive(dx)
        if dx > 0:
            multiply(dx - 1)
    swap(3).wait()

    def back(q, _):
        px = (x + q) % 4
        product = (total_ref[px] + partial(3, px)).astype(BF16)
        for h in range(2):
            for w in range(16):
                back_ref[px * 32 + h * 16 + w] = product[24 * w : 24 * w + 24, 128 * h : 128 * h + 128]

        def send(d, _):
            py, pz = (y + d // 8) % 4, (z + d % 8) % 8
            pltpu.make_async_remote_copy(
                src_ref=back_ref.at[px * 32 + py * 8 + pz], dst_ref=home_ref.at[me], send_sem=s_back, recv_sem=s_home,
                device_id=device_at(px, py, pz), device_id_type=MESH,
            ).start()
            return 0

        lax.fori_loop(jnp.where(q == 0, 1, 0), 32, send, 0)
        return 0

    lax.fori_loop(0, 4, back, 0)
    home_ref[me] = back_ref[me]
    others = pl.ds(0, CHIPS - 1)
    pltpu.make_async_copy(send_ref.at[others], send_ref.at[others], s_send).wait()
    pltpu.make_async_copy(home_ref.at[others], home_ref.at[others], s_home).wait()
    pltpu.make_async_copy(back_ref.at[others], back_ref.at[others], s_back).wait()

    def widen(c, _):
        sums_ref[pl.ds(pl.multiple_of(c * ROWS, 8), ROWS), :] = home_ref[c].astype(F32)
        return 0

    lax.fori_loop(0, CHIPS, widen, 0, unroll=4)

    def finish(i, _):
        values = sums_ref[pl.ds(i, CHIPS, stride=ROWS), :]
        mean = jnp.mean(values, axis=0, keepdims=True)
        centred = values - mean
        spread = jnp.mean(centred * centred, axis=0, keepdims=True)
        normed = (centred * lax.rsqrt(spread + EPS) * gain_ref[...] + bias_ref[...]).astype(BF16)
        projected = dot(normed, w_out_ref[...], 0, 0)
        natural = jnp.concatenate([projected[0:24], projected[48:72], projected[24:48], projected[72:96]], axis=0)
        out_ref[i] = (gate_ref[i] * natural).astype(BF16)
        return 0

    lax.fori_loop(0, ROWS, finish, 0, unroll=4)


def shards(pair, tile_mask, chain_ids, in_gain, in_bias, w_ab, w_gate, out_gain, out_bias, w_out):
    args = (
        pair, tile_mask, chain_ids.reshape(6, 128), in_gain.reshape(1, C), in_bias.reshape(1, C), w_ab, w_gate,
        out_gain.reshape(1, C), out_bias.reshape(1, C), w_out,
    )
    return pl.pallas_call(
        kernel,
        out_shape=jax.ShapeDtypeStruct((ROWS, COLS, C), BF16),
        in_specs=[pl.BlockSpec(memory_space=pl.ANY)] * len(args),
        out_specs=pl.BlockSpec(memory_space=pltpu.VMEM),
        scratch_shapes=[pltpu.VMEM(arg.shape, arg.dtype) for arg in args]
        + [
            pltpu.VMEM((ROWS, COLS, C), BF16),
            pltpu.VMEM((TILES, 128, C), BF16),
            pltpu.VMEM((TILES, 128), F32),
            pltpu.VMEM((512, C), BF16),
            pltpu.VMEM((32 * MSG, 128), F32),
            pltpu.VMEM((CHIPS, MSG, 128), BF16),
            pltpu.VMEM((CHIPS, MSG, 128), BF16),
            pltpu.VMEM((ROWS, COLS, C), F32),
            pltpu.VMEM((4, 384, 256), BF16),
            pltpu.VMEM((4, 8, 128, 256), BF16),
            pltpu.VMEM((4, 384, 256), F32),
            pltpu.VMEM((CHIPS, ROWS, 128), BF16),
            pltpu.VMEM((CHIPS, ROWS, 128), BF16),
            pltpu.VMEM((CHIPS * ROWS, 128), F32),
            pltpu.VMEM((C, 128), F32),
            pltpu.VMEM((C, 128), F32),
            pltpu.SemaphoreType.DMA((len(args),)),
            pltpu.SemaphoreType.REGULAR,
            pltpu.SemaphoreType.REGULAR,
            pltpu.SemaphoreType.DMA(()),
            pltpu.SemaphoreType.DMA((4,)),
            pltpu.SemaphoreType.DMA((4,)),
            pltpu.SemaphoreType.DMA((4,)),
            pltpu.SemaphoreType.DMA(()),
            pltpu.SemaphoreType.DMA(()),
        ],
        compiler_params=pltpu.CompilerParams(collective_id=1, has_side_effects=True, vmem_limit_bytes=60 << 20),
    )(*args)


def solution(mesh):
    in_specs = (P("wide", "narrow", None), P(), P(), P(), P(), P(), P(), P(), P(), P())
    out_specs = P("wide", "narrow", None)
    return jax.shard_map(shards, mesh=mesh, in_specs=in_specs, out_specs=out_specs, check_vma=False)
```

```python
import functools

import jax
import jax.numpy as jnp
from jax import lax
from jax.experimental import pallas as pl
from jax.experimental.pallas import tpu as pltpu
from jax.sharding import PartitionSpec as P

MESH = pl.DeviceIdType.MESH
F32, BF16 = jnp.float32, jnp.bfloat16
CHIPS = 128
ROWS, COLS, C = 24, 96, 128
MSG, SLOT = 36, 48
BACK, HOME = 18, 32
TILES = 18
EPS = 1e-05


def sigmoid(x):
    return 0.5 * jnp.tanh(0.5 * x) + 0.5


def dot(a, b, ca, cb):
    return lax.dot_general(a, b, (((ca,), (cb,)), ((), ())), preferred_element_type=F32)


def keep_mask(wide, narrow, tile_ref, chain_ref):
    tile = lax.broadcasted_iota(jnp.int32, (TILES, 128), 0)
    lane = lax.broadcasted_iota(jnp.int32, (TILES, 128), 1)
    body, main = tile < 16, lane < 96
    i = jnp.where(body, jnp.where(main, tile, 16 + tile % 8), 16 + 4 * (tile - 16) + lane // 32)
    k = jnp.where(body, jnp.where(main, lane, lane - 96 + 32 * (tile // 8)), 64 + lane % 32)
    i = i + wide * ROWS
    k = k + narrow * COLS
    chain_i = jnp.zeros((TILES, 128), jnp.int32)
    chain_k = jnp.zeros((TILES, 128), jnp.int32)
    chains = chain_ref[...]
    for q in range(1, 4):
        below = (chains < q).astype(F32)
        start = jnp.sum(jnp.sum(below, axis=0, keepdims=True), axis=1, keepdims=True).astype(jnp.int32)
        chain_i = chain_i + (i >= start).astype(jnp.int32)
        chain_k = chain_k + (k >= start).astype(jnp.int32)
    same = (chain_i == chain_k).astype(F32)
    row_tile, col_tile = i // 128, k // 128
    blocked = jnp.zeros((TILES, 128), F32)
    for a in range(6):
        in_row = row_tile == a
        for b in range(6):
            value = tile_ref[a : a + 1, b : b + 1].astype(F32)
            blocked = blocked + jnp.where(in_row & (col_tile == b), value, 0.0)
    return jnp.maximum(blocked, same)


def kernel(
    pair_hbm, tile_hbm, chain_hbm, in_gain_hbm, in_bias_hbm, w_ab_hbm, w_gate_hbm, out_gain_hbm, out_bias_hbm, w_out_hbm,
    out_ref,
    pair_ref, tile_ref, chain_ref, in_gain_ref, in_bias_ref, w_ab_ref, w_gate_ref, out_gain_ref, out_bias_ref, w_out_ref,
    normed_ref, packed_ref, mask_ref, w_t_ref, stage_ref, send_ref, recv_ref, gate_ref, a_ref, b_ref, total_ref, back_ref,
    home_ref, sums_ref, gain_ref, bias_ref,
    s_in, s_line, s_plane, s_send, s_recv, s_swap_send, s_swap_recv, s_back, s_home,
):
    wide, narrow = lax.axis_index("wide"), lax.axis_index("narrow")
    w16, core = wide // 2, wide % 2
    y_lo, z = wide // 16, w16 % 8
    x, y = narrow // 2, (narrow % 2) * 2 + y_lo
    me = x * 32 + y * 8 + z

    def device_at(px, py, pz):
        return ((py % 2) * 16 + pz * 2 + core, px * 2 + py // 2)

    sibling = (w16 * 2 + 1 - core, narrow)
    line_z = [device_at(x, y, (z + d) % 8) for d in range(1, 8)]
    line_y = [device_at(x, (y + d) % 4, z) for d in range(1, 4)]
    line_x = [device_at((x + d) % 4, y, z) for d in range(1, 4)]

    inputs = [
        pltpu.make_async_copy(source, target, s_in.at[at])
        for at, (source, target) in enumerate((
            (pair_hbm, pair_ref), (tile_hbm, tile_ref), (chain_hbm, chain_ref), (in_gain_hbm, in_gain_ref),
            (in_bias_hbm, in_bias_ref), (w_ab_hbm, w_ab_ref), (w_gate_hbm, w_gate_ref), (out_gain_hbm, out_gain_ref),
            (out_bias_hbm, out_bias_ref), (w_out_hbm, w_out_ref),
        ))
    ]
    for copy in inputs:
        copy.start()

    barrier = pltpu.get_barrier_semaphore()
    greeted = [sibling] + line_z + line_y + line_x
    for device in greeted:
        pl.semaphore_signal(barrier, inc=1, device_id=device, device_id_type=MESH)

    for copy in inputs:
        copy.wait()

    w_t_ref[...] = w_ab_ref[...].T
    mask_ref[...] = keep_mask(wide, narrow, tile_ref, chain_ref)
    gain_ref[...] = jnp.broadcast_to(out_gain_ref[...], (C, 128)).T
    bias_ref[...] = jnp.broadcast_to(out_bias_ref[...], (C, 128)).T

    pl.semaphore_wait(barrier, len(greeted))
    for device in line_y:
        pl.semaphore_signal(s_line, inc=1, device_id=device, device_id_type=MESH)

    def norm_row(i):
        values = pair_ref[i].astype(F32)
        mean = jnp.mean(values, axis=1, keepdims=True)
        centred = values - mean
        spread = jnp.mean(centred * centred, axis=1, keepdims=True)
        normed = (centred * lax.rsqrt(spread + EPS) * in_gain_ref[...] + in_bias_ref[...]).astype(BF16)
        normed_ref[i] = normed
        return normed

    def norm_body(i, _):
        packed_ref[i, 0:96] = norm_row(i)
        return 0

    def norm_tail(r, _):
        normed = norm_row(16 + r)
        packed_ref[r, 96:128] = normed[0:32]
        packed_ref[8 + r, 96:128] = normed[32:64]
        packed_ref[16 + r // 4, pl.ds(pl.multiple_of(32 * (r % 4), 32), 32)] = normed[64:96]
        return 0

    lax.fori_loop(0, 16, norm_body, 0, unroll=2)
    lax.fori_loop(0, 8, norm_tail, 0, unroll=2)

    pl.semaphore_wait(s_line, len(line_y))
    for device in line_x:
        pl.semaphore_signal(s_plane, inc=1, device_id=device, device_id_type=MESH)

    used = pl.ds(0, MSG)

    def send_chunk(dx):
        px = (x + dx) % 4
        first = pl.multiple_of(px * 32, 32)
        weights = jnp.concatenate([w_t_ref[pl.ds(g * 128 + first, 32), :] for g in range(4)], axis=0)

        def sides(t):
            proj = dot(weights, packed_ref[pl.ds(t, 2)].reshape(256, C), 1, 1)
            result = []
            for q in range(2):
                part = proj[:, 128 * q : 128 * q + 128]
                mask = mask_ref[pl.ds(t + q, 1), :]
                left = mask * sigmoid(part[0:32]) * part[32:64]
                right = mask * sigmoid(part[64:96]) * part[96:128]
                result.append((left, right))
            return result

        def project(h, _):
            t = 2 * h
            for q, (left, right) in enumerate(sides(t)):
                stage_ref[pl.ds(t + q, 32, stride=SLOT), :] = left
                stage_ref[pl.ds(16 + t + q, 32, stride=SLOT), :] = right
            return 0

        lax.fori_loop(0, 8, project, 0, unroll=2)
        for q, (left, right) in enumerate(sides(16)):
            stage_ref[pl.ds(32 + q, 32, stride=SLOT), :] = left
            stage_ref[pl.ds(34 + q, 32, stride=SLOT), :] = right

        def cast(c):
            start = pl.multiple_of(c * SLOT, 16)
            send_ref[px * 32 + c] = stage_ref[pl.ds(start, SLOT), :].astype(BF16)

        def send(d, _):
            py, pz = (y + d // 8) % 4, (z + d % 8) % 8
            slot = px * 32 + py * 8 + pz
            pltpu.make_async_remote_copy(
                src_ref=send_ref.at[slot, used], dst_ref=recv_ref.at[me, used], send_sem=s_send, recv_sem=s_recv.at[dx],
                device_id=device_at(px, py, pz), device_id_type=MESH,
            ).start()
            return 0

        def cast_body(c, _):
            cast(c)
            return 0

        lax.fori_loop(0, 32, cast_body, 0, unroll=4)
        if dx == 0:
            lax.fori_loop(1, 8, send, 0)
            lax.fori_loop(8, 32, send, 0)
            recv_ref[me] = send_ref[me]
        else:
            if dx == 1:
                pl.semaphore_wait(s_plane, len(line_x))
            lax.fori_loop(0, 32, send, 0)

    for dx in range(4):
        send_chunk(dx)

    def gates(i, _):
        gate_ref[i] = sigmoid(dot(normed_ref[i], w_gate_ref[...], 1, 0))
        return 0

    lax.fori_loop(0, ROWS, gates, 0)
    for dx in range(4):
        for p in range(8):
            b_ref[dx, p, 96:128] = jnp.zeros((32, 256), BF16)

    lane = lax.broadcasted_iota(jnp.int32, (8, 128), 1)
    row = lax.broadcasted_iota(jnp.int32, (8, 128), 0)

    def unpack(slot):
        f = recv_ref[slot].astype(F32)
        zero = jnp.zeros((8, 128), F32)

        def rest(top, middle, at):
            low = jnp.where(row < 4, f[at : at + 1], f[at + 1 : at + 2])
            turned = [pltpu.roll(low, 64, 1), pltpu.roll(low, 32, 1), low, pltpu.roll(low, 96, 1)]
            low = turned[3]
            for q in range(3):
                low = jnp.where(row % 4 == q, turned[q], low)
            return jnp.where(
                lane < 32, pltpu.roll(top, 32, 1),
                jnp.where(lane < 64, pltpu.roll(middle, 64, 1), jnp.where(lane < 96, low, zero)),
            )

        left = [jnp.where(lane < 96, f[0:8], zero), jnp.where(lane < 96, f[8:16], zero), rest(f[0:8], f[8:16], 32)]
        right = [f[16:24], f[24:32], rest(f[16:24], f[24:32], 34)]
        return left, right

    mine = pl.ds(pl.multiple_of(core * 48, 16), 48)

    def swap(dx):
        half = b_ref.at[dx, :, mine, :]
        return pltpu.make_async_remote_copy(
            src_ref=half, dst_ref=half, send_sem=s_swap_send.at[dx], recv_sem=s_swap_recv.at[dx], device_id=sibling,
            device_id_type=MESH,
        )

    def receive(dx):
        arrived = recv_ref.at[pl.ds(0, 31 if dx == 0 else 32), used]
        pltpu.make_async_copy(arrived, arrived, s_recv.at[dx]).wait()
        first = ((x + 4 - dx) % 4) * 32

        def assemble(p, _):
            for q in range(2):
                left0, right0 = unpack(first + 16 * q + 2 * p)
                left1, right1 = unpack(first + 16 * q + 2 * p + 1)
                columns = slice(128 * q, 128 * q + 128)
                rows = pl.ds(pl.multiple_of(p * 48, 16), 48)
                a_ref[dx, rows, columns] = jnp.concatenate(left0 + left1, axis=0).astype(BF16)
                b_ref[dx, p, mine, columns] = jnp.concatenate(right0 + right1, axis=0).astype(BF16)
            return 0

        lax.fori_loop(0, 8, assemble, 0)
        swap(dx).start()

    def partial(dx, px):
        return dot(a_ref[dx], b_ref[dx, pl.ds(2 * px, 2)].reshape(256, 256), 1, 1)

    def multiply(dx):
        swap(dx).wait()

        def step(px, _):
            if dx == 0:
                total_ref[px] = partial(dx, px)
            else:
                total_ref[px] += partial(dx, px)
            return 0

        lax.fori_loop(0, 4, step, 0)

    for dx in range(4):
        receive(dx)
        if dx > 0:
            multiply(dx - 1)
    swap(3).wait()

    def pack(block):
        extra = block[16:24]
        top = jnp.where(lane < 96, block[0:8], pltpu.roll(extra, 96, 1))
        middle = jnp.where(lane < 96, block[8:16], pltpu.roll(extra, 64, 1))
        turned = [pltpu.roll(extra, 64, 1), pltpu.roll(extra, 96, 1), extra, pltpu.roll(extra, 32, 1)]
        spread = jnp.zeros((8, 128), F32)
        for q in range(4):
            spread = jnp.where((row % 4 == q) & (lane // 32 == q), turned[q], spread)
        first = jnp.sum(spread[0:4], axis=0, keepdims=True)
        second = jnp.sum(spread[4:8], axis=0, keepdims=True)
        low = jnp.where(row == 0, first, second)
        return jnp.concatenate([top, middle, low, low], axis=0).astype(BF16)

    sent = pl.ds(0, BACK)

    def back(q, _):
        px = (x + q) % 4
        product = total_ref[px] + partial(3, px)
        for h in range(2):
            for w in range(16):
                back_ref[px * 32 + h * 16 + w] = pack(product[24 * w : 24 * w + 24, 128 * h : 128 * h + 128])

        def send(d, _):
            py, pz = (y + d // 8) % 4, (z + d % 8) % 8
            pltpu.make_async_remote_copy(
                src_ref=back_ref.at[px * 32 + py * 8 + pz, sent], dst_ref=home_ref.at[me, sent], send_sem=s_back, recv_sem=s_home,
                device_id=device_at(px, py, pz), device_id_type=MESH,
            ).start()
            return 0

        lax.fori_loop(jnp.where(q == 0, 1, 0), 32, send, 0)
        return 0

    lax.fori_loop(0, 4, back, 0)
    home_ref[me] = back_ref[me]
    others = pl.ds(0, CHIPS - 1)
    pltpu.make_async_copy(send_ref.at[others, used], send_ref.at[others, used], s_send).wait()
    pltpu.make_async_copy(home_ref.at[others, sent], home_ref.at[others, sent], s_home).wait()
    pltpu.make_async_copy(back_ref.at[others, sent], back_ref.at[others, sent], s_back).wait()

    def widen(c, _):
        sums_ref[pl.ds(pl.multiple_of(c * ROWS, 8), ROWS), :] = home_ref[c].astype(F32)[0:ROWS]
        return 0

    lax.fori_loop(0, CHIPS, widen, 0, unroll=4)

    lanes = lax.broadcasted_iota(jnp.int32, (CHIPS, 128), 1)

    def rows_at(at):
        return sums_ref[pl.ds(at, CHIPS, stride=ROWS), :]

    def finish_main(i, _):
        finish(i, rows_at(i))
        return 0

    def finish_rest(r, q):
        low = rows_at(16 + r // 4)
        shift = (64 - 32 * q) % 128
        low = pltpu.roll(low, shift, 1) if shift else low
        high = jnp.where(lanes < 32, pltpu.roll(rows_at(r), 32, 1), pltpu.roll(rows_at(8 + r), 64, 1))
        finish(16 + r, jnp.where(lanes < 64, high, low))

    def finish(i, values):
        mean = jnp.mean(values, axis=0, keepdims=True)
        centred = values - mean
        spread = jnp.mean(centred * centred, axis=0, keepdims=True)
        normed = (centred * lax.rsqrt(spread + EPS) * gain_ref[...] + bias_ref[...]).astype(BF16)
        projected = dot(normed, w_out_ref[...], 0, 0)
        natural = jnp.concatenate([projected[0:24], projected[48:72], projected[24:48], projected[72:96]], axis=0)
        out_ref[i] = (gate_ref[i] * natural).astype(BF16)

    lax.fori_loop(0, 16, finish_main, 0, unroll=4)

    def finish_four(h, _):
        for q in range(4):
            finish_rest(4 * h + q, q)
        return 0

    lax.fori_loop(0, 2, finish_four, 0)


def shards(pair, tile_mask, chain_ids, in_gain, in_bias, w_ab, w_gate, out_gain, out_bias, w_out):
    args = (
        pair, tile_mask, chain_ids.reshape(6, 128), in_gain.reshape(1, C), in_bias.reshape(1, C), w_ab, w_gate,
        out_gain.reshape(1, C), out_bias.reshape(1, C), w_out,
    )
    return pl.pallas_call(
        kernel,
        out_shape=jax.ShapeDtypeStruct((ROWS, COLS, C), BF16),
        in_specs=[pl.BlockSpec(memory_space=pltpu.HBM)] * len(args),
        out_specs=pl.BlockSpec(memory_space=pltpu.VMEM),
        scratch_shapes=[pltpu.VMEM(arg.shape, arg.dtype) for arg in args]
        + [
            pltpu.VMEM((ROWS, COLS, C), BF16),
            pltpu.VMEM((TILES, 128, C), BF16),
            pltpu.VMEM((TILES, 128), F32),
            pltpu.VMEM((512, C), BF16),
            pltpu.VMEM((32 * SLOT, 128), F32),
            pltpu.VMEM((CHIPS, SLOT, 128), BF16),
            pltpu.VMEM((CHIPS, SLOT, 128), BF16),
            pltpu.VMEM((ROWS, COLS, C), F32),
            pltpu.VMEM((4, 384, 256), BF16),
            pltpu.VMEM((4, 8, 128, 256), BF16),
            pltpu.VMEM((4, 384, 256), F32),
            pltpu.VMEM((CHIPS, HOME, 128), BF16),
            pltpu.VMEM((CHIPS, HOME, 128), BF16),
            pltpu.VMEM((CHIPS * ROWS, 128), F32),
            pltpu.VMEM((C, 128), F32),
            pltpu.VMEM((C, 128), F32),
            pltpu.SemaphoreType.DMA((len(args),)),
            pltpu.SemaphoreType.REGULAR,
            pltpu.SemaphoreType.REGULAR,
            pltpu.SemaphoreType.DMA(()),
            pltpu.SemaphoreType.DMA((4,)),
            pltpu.SemaphoreType.DMA((4,)),
            pltpu.SemaphoreType.DMA((4,)),
            pltpu.SemaphoreType.DMA(()),
            pltpu.SemaphoreType.DMA(()),
        ],
        compiler_params=pltpu.CompilerParams(collective_id=1, has_side_effects=True, vmem_limit_bytes=60 << 20),
    )(*args)


def solution(mesh):
    in_specs = (P("wide", "narrow", None), P(), P(), P(), P(), P(), P(), P(), P(), P())
    out_specs = P("wide", "narrow", None)
    return jax.shard_map(shards, mesh=mesh, in_specs=in_specs, out_specs=out_specs, check_vma=False)
```

```python
import functools

import jax
import jax.numpy as jnp
from jax import lax
from jax.experimental import pallas as pl
from jax.experimental.pallas import tpu as pltpu
from jax.sharding import PartitionSpec as P

MESH = pl.DeviceIdType.MESH
F32, BF16 = jnp.float32, jnp.bfloat16
CHIPS = 128
ROWS, COLS, C = 24, 96, 128
MSG, SLOT = 36, 48
BACK, HOME = 18, 32
TILES = 18
EPS = 1e-05


def sigmoid(x):
    return 0.5 * jnp.tanh(0.5 * x) + 0.5


def dot(a, b, ca, cb):
    return lax.dot_general(a, b, (((ca,), (cb,)), ((), ())), preferred_element_type=F32)


def keep_mask(wide, narrow, tile_ref, chain_ref):
    tile = lax.broadcasted_iota(jnp.int32, (TILES, 128), 0)
    lane = lax.broadcasted_iota(jnp.int32, (TILES, 128), 1)
    body, main = tile < 16, lane < 96
    i = jnp.where(body, jnp.where(main, tile, 16 + tile % 8), 16 + 4 * (tile - 16) + lane // 32)
    k = jnp.where(body, jnp.where(main, lane, lane - 96 + 32 * (tile // 8)), 64 + lane % 32)
    i = i + wide * ROWS
    k = k + narrow * COLS
    chain_i = jnp.zeros((TILES, 128), jnp.int32)
    chain_k = jnp.zeros((TILES, 128), jnp.int32)
    chains = chain_ref[...]
    for q in range(1, 4):
        below = (chains < q).astype(F32)
        start = jnp.sum(jnp.sum(below, axis=0, keepdims=True), axis=1, keepdims=True).astype(jnp.int32)
        chain_i = chain_i + (i >= start).astype(jnp.int32)
        chain_k = chain_k + (k >= start).astype(jnp.int32)
    same = (chain_i == chain_k).astype(F32)
    row_tile, col_tile = i // 128, k // 128
    blocked = jnp.zeros((TILES, 128), F32)
    for a in range(6):
        in_row = row_tile == a
        for b in range(6):
            value = tile_ref[a : a + 1, b : b + 1].astype(F32)
            blocked = blocked + jnp.where(in_row & (col_tile == b), value, 0.0)
    return jnp.maximum(blocked, same)


def kernel(
    pair_hbm, tile_hbm, chain_hbm, in_gain_hbm, in_bias_hbm, w_ab_hbm, w_gate_hbm, out_gain_hbm, out_bias_hbm, w_out_hbm,
    out_ref,
    pair_ref, tile_ref, chain_ref, in_gain_ref, in_bias_ref, w_ab_ref, w_gate_ref, out_gain_ref, out_bias_ref, w_out_ref,
    normed_ref, packed_ref, mask_ref, w_t_ref, stage_ref, send_ref, recv_ref, gate_ref, a_ref, b_ref, total_ref, back_ref,
    home_ref, sums_ref, gain_ref, bias_ref,
    s_in, s_line, s_plane, s_send, s_recv, s_swap_send, s_swap_recv, s_back, s_home,
):
    wide, narrow = lax.axis_index("wide"), lax.axis_index("narrow")
    w16, core = wide // 2, wide % 2
    y_lo, z = wide // 16, w16 % 8
    x, y = narrow // 2, (narrow % 2) * 2 + y_lo
    me = x * 32 + y * 8 + z

    def device_at(px, py, pz):
        return ((py % 2) * 16 + pz * 2 + core, px * 2 + py // 2)

    sibling = (w16 * 2 + 1 - core, narrow)
    line_z = [device_at(x, y, (z + d) % 8) for d in range(1, 8)]
    line_y = [device_at(x, (y + d) % 4, z) for d in range(1, 4)]
    line_x = [device_at((x + d) % 4, y, z) for d in range(1, 4)]

    inputs = [
        pltpu.make_async_copy(source, target, s_in.at[at])
        for at, (source, target) in enumerate((
            (pair_hbm, pair_ref), (tile_hbm, tile_ref), (chain_hbm, chain_ref), (in_gain_hbm, in_gain_ref),
            (in_bias_hbm, in_bias_ref), (w_ab_hbm, w_ab_ref), (w_gate_hbm, w_gate_ref), (out_gain_hbm, out_gain_ref),
            (out_bias_hbm, out_bias_ref), (w_out_hbm, w_out_ref),
        ))
    ]
    for copy in inputs:
        copy.start()

    barrier = pltpu.get_barrier_semaphore()
    greeted = [sibling] + line_z + line_y + line_x
    for device in greeted:
        pl.semaphore_signal(barrier, inc=1, device_id=device, device_id_type=MESH)

    for copy in inputs:
        copy.wait()

    w_t_ref[...] = w_ab_ref[...].T
    mask_ref[...] = keep_mask(wide, narrow, tile_ref, chain_ref)
    ones = jnp.ones((C, 128), BF16)

    def norm_row(i):
        values = pair_ref[i].astype(F32)
        mean = dot(pair_ref[i], ones, 1, 0) * (1.0 / C)
        centred = values - mean
        spread = jnp.mean(centred * centred, axis=1, keepdims=True)
        normed = (centred * lax.rsqrt(spread + EPS) * in_gain_ref[...] + in_bias_ref[...]).astype(BF16)
        normed_ref[i] = normed
        return normed

    def norm_body(i, _):
        packed_ref[i, 0:96] = norm_row(i)
        return 0

    def norm_tail(r, _):
        normed = norm_row(16 + r)
        packed_ref[r, 96:128] = normed[0:32]
        packed_ref[8 + r, 96:128] = normed[32:64]
        packed_ref[16 + r // 4, pl.ds(pl.multiple_of(32 * (r % 4), 32), 32)] = normed[64:96]
        return 0

    lax.fori_loop(0, 16, norm_body, 0, unroll=4)
    lax.fori_loop(0, 8, norm_tail, 0, unroll=4)

    pl.semaphore_wait(barrier, len(greeted))
    for device in line_y:
        pl.semaphore_signal(s_line, inc=1, device_id=device, device_id_type=MESH)

    used = pl.ds(0, MSG)

    def send_chunk(dx):
        px = (x + dx) % 4
        first = pl.multiple_of(px * 32, 32)
        weights = jnp.concatenate([w_t_ref[pl.ds(g * 128 + first, 32), :] for g in range(4)], axis=0)

        def sides(t):
            proj = dot(weights, packed_ref[pl.ds(t, 2)].reshape(256, C), 1, 1)
            result = []
            for q in range(2):
                part = proj[:, 128 * q : 128 * q + 128]
                mask = mask_ref[pl.ds(t + q, 1), :]
                left = mask * sigmoid(part[0:32]) * part[32:64]
                right = mask * sigmoid(part[64:96]) * part[96:128]
                result.append((left, right))
            return result

        def project(h, _):
            t = 2 * h
            for q, (left, right) in enumerate(sides(t)):
                stage_ref[pl.ds(t + q, 32, stride=SLOT), :] = left
                stage_ref[pl.ds(16 + t + q, 32, stride=SLOT), :] = right
            return 0

        lax.fori_loop(0, 8, project, 0, unroll=2)
        for q, (left, right) in enumerate(sides(16)):
            stage_ref[pl.ds(32 + q, 32, stride=SLOT), :] = left
            stage_ref[pl.ds(34 + q, 32, stride=SLOT), :] = right

        def cast(c):
            start = pl.multiple_of(c * SLOT, 16)
            send_ref[px * 32 + c] = stage_ref[pl.ds(start, SLOT), :].astype(BF16)

        def send(d, _):
            py, pz = (y + d // 8) % 4, (z + d % 8) % 8
            slot = px * 32 + py * 8 + pz
            pltpu.make_async_remote_copy(
                src_ref=send_ref.at[slot, used], dst_ref=recv_ref.at[me, used], send_sem=s_send, recv_sem=s_recv.at[dx],
                device_id=device_at(px, py, pz), device_id_type=MESH,
            ).start()
            return 0

        def cast_body(c, _):
            cast(c)
            return 0

        lax.fori_loop(0, 32, cast_body, 0, unroll=4)
        if dx == 0:
            lax.fori_loop(1, 8, send, 0)
            pl.semaphore_wait(s_line, len(line_y))
            for device in line_x:
                pl.semaphore_signal(s_plane, inc=1, device_id=device, device_id_type=MESH)
            lax.fori_loop(8, 32, send, 0)
            recv_ref[me] = send_ref[me]
        else:
            if dx == 1:
                pl.semaphore_wait(s_plane, len(line_x))
            lax.fori_loop(0, 32, send, 0)

    for dx in range(4):
        send_chunk(dx)

    def gates(i, _):
        gate_ref[i] = sigmoid(dot(normed_ref[i], w_gate_ref[...], 1, 0))
        return 0

    lax.fori_loop(0, ROWS, gates, 0, unroll=2)
    gain_ref[...] = jnp.broadcast_to(out_gain_ref[...], (C, 128)).T
    bias_ref[...] = jnp.broadcast_to(out_bias_ref[...], (C, 128)).T
    for dx in range(4):
        for p in range(8):
            b_ref[dx, p, 96:128] = jnp.zeros((32, 256), BF16)

    lane = lax.broadcasted_iota(jnp.int32, (8, 128), 1)
    row = lax.broadcasted_iota(jnp.int32, (8, 128), 0)

    def unpack(slot):
        f = recv_ref[slot].astype(F32)
        zero = jnp.zeros((8, 128), F32)

        def rest(top, middle, at):
            low = jnp.where(row < 4, f[at : at + 1], f[at + 1 : at + 2])
            turned = [pltpu.roll(low, 64, 1), pltpu.roll(low, 32, 1), low, pltpu.roll(low, 96, 1)]
            low = turned[3]
            for q in range(3):
                low = jnp.where(row % 4 == q, turned[q], low)
            return jnp.where(
                lane < 32, pltpu.roll(top, 32, 1),
                jnp.where(lane < 64, pltpu.roll(middle, 64, 1), jnp.where(lane < 96, low, zero)),
            )

        left = [jnp.where(lane < 96, f[0:8], zero), jnp.where(lane < 96, f[8:16], zero), rest(f[0:8], f[8:16], 32)]
        right = [f[16:24], f[24:32], rest(f[16:24], f[24:32], 34)]
        return left, right

    mine = pl.ds(pl.multiple_of(core * 48, 16), 48)

    def swap(dx):
        half = b_ref.at[dx, :, mine, :]
        return pltpu.make_async_remote_copy(
            src_ref=half, dst_ref=half, send_sem=s_swap_send.at[dx], recv_sem=s_swap_recv.at[dx], device_id=sibling,
            device_id_type=MESH,
        )

    def receive(dx):
        arrived = recv_ref.at[pl.ds(0, 31 if dx == 0 else 32), used]
        pltpu.make_async_copy(arrived, arrived, s_recv.at[dx]).wait()
        first = ((x + 4 - dx) % 4) * 32

        def assemble(p, _):
            for q in range(2):
                left0, right0 = unpack(first + 16 * q + 2 * p)
                left1, right1 = unpack(first + 16 * q + 2 * p + 1)
                columns = slice(128 * q, 128 * q + 128)
                rows = pl.ds(pl.multiple_of(p * 48, 16), 48)
                a_ref[dx, rows, columns] = jnp.concatenate(left0 + left1, axis=0).astype(BF16)
                b_ref[dx, p, mine, columns] = jnp.concatenate(right0 + right1, axis=0).astype(BF16)
            return 0

        lax.fori_loop(0, 8, assemble, 0)
        swap(dx).start()

    def partial(dx, px):
        return dot(a_ref[dx], b_ref[dx, pl.ds(2 * px, 2)].reshape(256, 256), 1, 1)

    def multiply(dx):
        swap(dx).wait()

        def step(px, _):
            if dx == 0:
                total_ref[px] = partial(dx, px)
            else:
                total_ref[px] += partial(dx, px)
            return 0

        lax.fori_loop(0, 4, step, 0)

    for dx in range(4):
        receive(dx)
        if dx > 0:
            multiply(dx - 1)
    swap(3).wait()

    def pack(block):
        extra = block[16:24]
        top = jnp.where(lane < 96, block[0:8], pltpu.roll(extra, 96, 1))
        middle = jnp.where(lane < 96, block[8:16], pltpu.roll(extra, 64, 1))
        turned = [pltpu.roll(extra, 64, 1), pltpu.roll(extra, 96, 1), extra, pltpu.roll(extra, 32, 1)]
        spread = jnp.zeros((8, 128), F32)
        for q in range(4):
            spread = jnp.where((row % 4 == q) & (lane // 32 == q), turned[q], spread)
        first = jnp.sum(spread[0:4], axis=0, keepdims=True)
        second = jnp.sum(spread[4:8], axis=0, keepdims=True)
        low = jnp.where(row == 0, first, second)
        return jnp.concatenate([top, middle, low, low], axis=0).astype(BF16)

    sent = pl.ds(0, BACK)

    def back(q, _):
        px = (x + q) % 4
        product = total_ref[px] + partial(3, px)
        for h in range(2):
            for w in range(16):
                back_ref[px * 32 + h * 16 + w] = pack(product[24 * w : 24 * w + 24, 128 * h : 128 * h + 128])

        def send(d, _):
            py, pz = (y + d // 8) % 4, (z + d % 8) % 8
            pltpu.make_async_remote_copy(
                src_ref=back_ref.at[px * 32 + py * 8 + pz, sent], dst_ref=home_ref.at[me, sent], send_sem=s_back, recv_sem=s_home.at[q],
                device_id=device_at(px, py, pz), device_id_type=MESH,
            ).start()
            return 0

        lax.fori_loop(jnp.where(q == 0, 1, 0), 32, send, 0)
        return 0

    lax.fori_loop(0, 4, back, 0)
    home_ref[me] = back_ref[me]
    others = pl.ds(0, CHIPS - 1)
    pltpu.make_async_copy(send_ref.at[others, used], send_ref.at[others, used], s_send).wait()

    def widen(c, _):
        sums_ref[pl.ds(pl.multiple_of(c * ROWS, 8), ROWS), :] = home_ref[c].astype(F32)[0:ROWS]
        return 0

    for q in range(4):
        arrived = home_ref.at[pl.ds(0, 31 if q == 0 else 32), sent]
        pltpu.make_async_copy(arrived, arrived, s_home.at[q]).wait()
        first = ((x + 4 - q) % 4) * 32
        lax.fori_loop(0, 32, lambda c, _, first=first: widen(first + c, _), 0, unroll=4)

    lanes = lax.broadcasted_iota(jnp.int32, (CHIPS, 128), 1)

    def rows_at(at):
        return sums_ref[pl.ds(at, CHIPS, stride=ROWS), :]

    def finish_main(i, _):
        finish(i, rows_at(i))
        return 0

    def finish_rest(r, q):
        low = rows_at(16 + r // 4)
        shift = (64 - 32 * q) % 128
        low = pltpu.roll(low, shift, 1) if shift else low
        high = jnp.where(lanes < 32, pltpu.roll(rows_at(r), 32, 1), pltpu.roll(rows_at(8 + r), 64, 1))
        finish(16 + r, jnp.where(lanes < 64, high, low))

    def finish(i, values):
        mean = jnp.mean(values, axis=0, keepdims=True)
        centred = values - mean
        spread = jnp.mean(centred * centred, axis=0, keepdims=True)
        normed = (centred * lax.rsqrt(spread + EPS) * gain_ref[...] + bias_ref[...]).astype(BF16)
        projected = dot(normed, w_out_ref[...], 0, 0)
        natural = jnp.concatenate([projected[0:24], projected[48:72], projected[24:48], projected[72:96]], axis=0)
        out_ref[i] = (gate_ref[i] * natural).astype(BF16)

    lax.fori_loop(0, 16, finish_main, 0, unroll=4)

    def finish_four(h, _):
        for q in range(4):
            finish_rest(4 * h + q, q)
        return 0

    lax.fori_loop(0, 2, finish_four, 0)
    pltpu.make_async_copy(back_ref.at[others, sent], back_ref.at[others, sent], s_back).wait()


def shards(pair, tile_mask, chain_ids, in_gain, in_bias, w_ab, w_gate, out_gain, out_bias, w_out):
    args = (
        pair, tile_mask, chain_ids.reshape(6, 128), in_gain.reshape(1, C), in_bias.reshape(1, C), w_ab, w_gate,
        out_gain.reshape(1, C), out_bias.reshape(1, C), w_out,
    )
    args = tuple(pltpu.with_memory_space_constraint(arg, pltpu.HBM) for arg in args)
    return pl.pallas_call(
        kernel,
        out_shape=pltpu.VMEM((ROWS, COLS, C), BF16),
        in_specs=[pl.BlockSpec(memory_space=pltpu.HBM)] * len(args),
        out_specs=pl.BlockSpec(memory_space=pltpu.VMEM),
        scratch_shapes=[pltpu.VMEM(arg.shape, arg.dtype) for arg in args]
        + [
            pltpu.VMEM((ROWS, COLS, C), BF16),
            pltpu.VMEM((TILES, 128, C), BF16),
            pltpu.VMEM((TILES, 128), F32),
            pltpu.VMEM((512, C), BF16),
            pltpu.VMEM((32 * SLOT, 128), F32),
            pltpu.VMEM((CHIPS, SLOT, 128), BF16),
            pltpu.VMEM((CHIPS, SLOT, 128), BF16),
            pltpu.VMEM((ROWS, COLS, C), F32),
            pltpu.VMEM((4, 384, 256), BF16),
            pltpu.VMEM((4, 8, 128, 256), BF16),
            pltpu.VMEM((4, 384, 256), F32),
            pltpu.VMEM((CHIPS, HOME, 128), BF16),
            pltpu.VMEM((CHIPS, HOME, 128), BF16),
            pltpu.VMEM((CHIPS * ROWS, 128), F32),
            pltpu.VMEM((C, 128), F32),
            pltpu.VMEM((C, 128), F32),
            pltpu.SemaphoreType.DMA((len(args),)),
            pltpu.SemaphoreType.REGULAR,
            pltpu.SemaphoreType.REGULAR,
            pltpu.SemaphoreType.DMA(()),
            pltpu.SemaphoreType.DMA((4,)),
            pltpu.SemaphoreType.DMA((4,)),
            pltpu.SemaphoreType.DMA((4,)),
            pltpu.SemaphoreType.DMA(()),
            pltpu.SemaphoreType.DMA((4,)),
        ],
        compiler_params=pltpu.CompilerParams(collective_id=1, has_side_effects=True, vmem_limit_bytes=40 << 20),
    )(*args)


def solution(mesh):
    in_specs = (P("wide", "narrow", None), P(), P(), P(), P(), P(), P(), P(), P(), P())
    out_specs = P("wide", "narrow", None)
    return jax.shard_map(shards, mesh=mesh, in_specs=in_specs, out_specs=out_specs, check_vma=False)
```

```python
import functools

import jax
import jax.numpy as jnp
from jax import lax
from jax.experimental import pallas as pl
from jax.experimental.pallas import tpu as pltpu
from jax.sharding import PartitionSpec as P

MESH = pl.DeviceIdType.MESH
F32, BF16 = jnp.float32, jnp.bfloat16
CHIPS = 128
ROWS, COLS, C = 24, 96, 128
MSG, SLOT, STAGE = 18, 32, 48
TILES = 18
PAIRS = ((3, 5), (0, 4), (2, 6), (1, 7))
EPS = 1e-05


def sigmoid(x):
    return 0.5 * jnp.tanh(0.5 * x) + 0.5


def dot(a, b, ca, cb):
    return lax.dot_general(a, b, (((ca,), (cb,)), ((), ())), preferred_element_type=F32)


def keep_mask(wide, narrow, tile_ref, chain_ref):
    tile = lax.broadcasted_iota(jnp.int32, (TILES, 128), 0)
    lane = lax.broadcasted_iota(jnp.int32, (TILES, 128), 1)
    body, main = tile < 16, lane < 96
    i = jnp.where(body, jnp.where(main, tile, 16 + tile % 8), 16 + 4 * (tile - 16) + lane // 32)
    k = jnp.where(body, jnp.where(main, lane, lane - 96 + 32 * (tile // 8)), 64 + lane % 32)
    i = i + wide * ROWS
    k = k + narrow * COLS
    chain_i = jnp.zeros((TILES, 128), jnp.int32)
    chain_k = jnp.zeros((TILES, 128), jnp.int32)
    chains = chain_ref[...]
    for q in range(1, 4):
        below = (chains < q).astype(F32)
        start = jnp.sum(jnp.sum(below, axis=0, keepdims=True), axis=1, keepdims=True).astype(jnp.int32)
        chain_i = chain_i + (i >= start).astype(jnp.int32)
        chain_k = chain_k + (k >= start).astype(jnp.int32)
    same = (chain_i == chain_k).astype(F32)
    row_tile, col_tile = i // 128, k // 128
    blocked = jnp.zeros((TILES, 128), F32)
    for a in range(6):
        in_row = row_tile == a
        for b in range(6):
            value = tile_ref[a : a + 1, b : b + 1].astype(F32)
            blocked = blocked + jnp.where(in_row & (col_tile == b), value, 0.0)
    return jnp.maximum(blocked, same)


def kernel(
    pair_hbm, tile_hbm, chain_hbm, in_gain_hbm, in_bias_hbm, w_ab_hbm, w_gate_hbm, out_gain_hbm, out_bias_hbm, w_out_hbm,
    out_ref,
    pair_ref, tile_ref, chain_ref, in_gain_ref, in_bias_ref, w_ab_ref, w_gate_ref, out_gain_ref, out_bias_ref, w_out_ref,
    normed_ref, packed_ref, mask_ref, w_t_ref, stage_ref, left_out, right_out, left_in, right_in, gate_ref, a_ref, b_ref,
    back_ref, home_ref, sums_ref, gain_ref, bias_ref,
    s_in, s_line, s_plane, s_left_out, s_right_out, s_left_in, s_right_in, s_swap_send, s_swap_recv, s_back, s_home,
):
    wide, narrow = lax.axis_index("wide"), lax.axis_index("narrow")
    w16, core = wide // 2, wide % 2
    y_lo, z = wide // 16, w16 % 8
    x, y = narrow // 2, (narrow % 2) * 2 + y_lo
    me = x * 32 + y * 8 + z

    def device_at(px, py, pz):
        return ((py % 2) * 16 + pz * 2 + core, px * 2 + py // 2)

    sibling = (w16 * 2 + 1 - core, narrow)
    line_z = [device_at(x, y, (z + d) % 8) for d in range(1, 8)]
    line_y = [device_at(x, (y + d) % 4, z) for d in range(1, 4)]
    line_x = [device_at((x + d) % 4, y, z) for d in range(1, 4)]

    inputs = [
        pltpu.make_async_copy(source, target, s_in.at[at])
        for at, (source, target) in enumerate((
            (pair_hbm, pair_ref), (tile_hbm, tile_ref), (chain_hbm, chain_ref), (in_gain_hbm, in_gain_ref),
            (in_bias_hbm, in_bias_ref), (w_ab_hbm, w_ab_ref), (w_gate_hbm, w_gate_ref), (out_gain_hbm, out_gain_ref),
            (out_bias_hbm, out_bias_ref), (w_out_hbm, w_out_ref),
        ))
    ]
    for copy in inputs:
        copy.start()

    barrier = pltpu.get_barrier_semaphore()
    greeted = [sibling] + line_z + line_y + line_x
    for device in greeted:
        pl.semaphore_signal(barrier, inc=1, device_id=device, device_id_type=MESH)

    for copy in inputs:
        copy.wait()

    w_t_ref[...] = w_ab_ref[...].T
    mask_ref[...] = keep_mask(wide, narrow, tile_ref, chain_ref)
    ones = jnp.ones((C, 128), BF16)

    def norm_row(i):
        values = pair_ref[i].astype(F32)
        mean = dot(pair_ref[i], ones, 1, 0) * (1.0 / C)
        centred = values - mean
        spread = jnp.mean(centred * centred, axis=1, keepdims=True)
        normed = (centred * lax.rsqrt(spread + EPS) * in_gain_ref[...] + in_bias_ref[...]).astype(BF16)
        normed_ref[i] = normed
        return normed

    def norm_body(i, _):
        packed_ref[i, 0:96] = norm_row(i)
        return 0

    def norm_tail(r, _):
        normed = norm_row(16 + r)
        packed_ref[r, 96:128] = normed[0:32]
        packed_ref[8 + r, 96:128] = normed[32:64]
        packed_ref[16 + r // 4, pl.ds(pl.multiple_of(32 * (r % 4), 32), 32)] = normed[64:96]
        return 0

    lax.fori_loop(0, 16, norm_body, 0, unroll=4)
    lax.fori_loop(0, 8, norm_tail, 0, unroll=4)

    pl.semaphore_wait(barrier, len(greeted))
    for device in line_y:
        pl.semaphore_signal(s_line, inc=1, device_id=device, device_id_type=MESH)

    used = pl.ds(0, MSG)

    def send_chunk(dx):
        px = (x + dx) % 4
        first = pl.multiple_of(px * 32, 32)
        weights = jnp.concatenate([w_t_ref[pl.ds(g * 128 + first, 32), :] for g in range(4)], axis=0)

        def sides(t):
            proj = dot(weights, packed_ref[pl.ds(t, 2)].reshape(256, C), 1, 1)
            result = []
            for q in range(2):
                part = proj[:, 128 * q : 128 * q + 128]
                mask = mask_ref[pl.ds(t + q, 1), :]
                left = mask * sigmoid(part[0:32]) * part[32:64]
                right = mask * sigmoid(part[64:96]) * part[96:128]
                result.append((left, right))
            return result

        def project(h, _):
            t = 2 * h
            for q, (left, right) in enumerate(sides(t)):
                stage_ref[pl.ds(t + q, 32, stride=STAGE), :] = left
                stage_ref[pl.ds(24 + t + q, 32, stride=STAGE), :] = right
            return 0

        lax.fori_loop(0, TILES // 2, project, 0, unroll=3)

        def cast(c):
            start = pl.multiple_of(c * STAGE, 16)
            both = stage_ref[pl.ds(start, STAGE), :]
            left_out[px * 32 + c] = both[0:32].astype(BF16)
            right_out[px * 32 + c] = jnp.concatenate([both[24:48], both[40:48]], axis=0).astype(BF16)

        def send(d, _):
            py, pz = (y + d // 8) % 4, (z + d % 8) % 8
            pltpu.make_async_remote_copy(
                src_ref=right_out.at[px * 32 + py * 8 + pz, used], dst_ref=right_in.at[me, used], send_sem=s_right_out,
                recv_sem=s_right_in.at[dx], device_id=device_at(px, py, pz), device_id_type=MESH,
            ).start()
            return 0

        def cast_body(c, _):
            cast(c)
            return 0

        lax.fori_loop(0, 32, cast_body, 0, unroll=4)
        if dx == 0:
            lax.fori_loop(1, 8, send, 0)
            pl.semaphore_wait(s_line, len(line_y))
            for device in line_x:
                pl.semaphore_signal(s_plane, inc=1, device_id=device, device_id_type=MESH)
            lax.fori_loop(8, 32, send, 0)
        else:
            if dx == 1:
                pl.semaphore_wait(s_plane, len(line_x))
            lax.fori_loop(0, 32, send, 0)

    for dx in range(4):
        send_chunk(dx)

    def send_pair(source, target, s_out, s_in_pair, pair, sign):
        for dz in pair:
            pz = (z + sign * dz + 8) % 8

            def send(r, _, pz=pz):
                px, py = (x + r // 4) % 4, (y + r % 4) % 4
                pltpu.make_async_remote_copy(
                    src_ref=source.at[px * 32 + py * 8 + pz, used], dst_ref=target.at[me, used], send_sem=s_out,
                    recv_sem=s_in_pair, device_id=device_at(px, py, pz), device_id_type=MESH,
                ).start()
                return 0

            lax.fori_loop(1 if dz == 0 else 0, 16, send, 0)

    for at, pair in enumerate(PAIRS):
        send_pair(left_out, left_in, s_left_out, s_left_in.at[at], pair, 1)
    left_in[me] = left_out[me]
    right_in[me] = right_out[me]

    def gates(i, _):
        gate_ref[i] = sigmoid(dot(normed_ref[i], w_gate_ref[...], 1, 0))
        return 0

    lax.fori_loop(0, ROWS, gates, 0, unroll=2)
    gain_ref[...] = jnp.broadcast_to(out_gain_ref[...], (C, 128)).T
    bias_ref[...] = jnp.broadcast_to(out_bias_ref[...], (C, 128)).T
    for p in range(8):
        b_ref[p, 96:128] = jnp.zeros((32, 1024), BF16)

    lane = lax.broadcasted_iota(jnp.int32, (8, 128), 1)
    row = lax.broadcasted_iota(jnp.int32, (8, 128), 0)

    def unpack(ref, slot, last):
        f = ref[slot].astype(F32)
        low = jnp.where(row < 4, f[16:17], f[17:18])
        turned = [pltpu.roll(low, 64, 1), pltpu.roll(low, 32, 1), low, pltpu.roll(low, 96, 1)]
        low = turned[3]
        for q in range(3):
            low = jnp.where(row % 4 == q, turned[q], low)
        rest = jnp.where(lane < 32, pltpu.roll(f[0:8], 32, 1), jnp.where(lane < 64, pltpu.roll(f[8:16], 64, 1), low))
        if last:
            return [f[0:8], f[8:16], rest]
        zero = jnp.zeros((8, 128), F32)
        return [jnp.where(lane < 96, part, zero) for part in (f[0:8], f[8:16], rest)]

    mine = pl.ds(pl.multiple_of(core * 48, 16), 48)

    def swap(dx):
        half = b_ref.at[:, mine, 256 * dx : 256 * dx + 256]
        return pltpu.make_async_remote_copy(
            src_ref=half, dst_ref=half, send_sem=s_swap_send.at[dx], recv_sem=s_swap_recv.at[dx], device_id=sibling,
            device_id_type=MESH,
        )

    def receive_right(dx):
        arrived = right_in.at[pl.ds(0, 31 if dx == 0 else 32), used]
        pltpu.make_async_copy(arrived, arrived, s_right_in.at[dx]).wait()
        first = ((x + 4 - dx) % 4) * 32

        def assemble(p, _):
            for q in range(2):
                right0 = unpack(right_in, first + 16 * q + 2 * p, True)
                right1 = unpack(right_in, first + 16 * q + 2 * p + 1, True)
                columns = slice(256 * dx + 128 * q, 256 * dx + 128 * q + 128)
                b_ref[p, mine, columns] = jnp.concatenate(right0 + right1, axis=0).astype(BF16)
            return 0

        lax.fori_loop(0, 8, assemble, 0)
        swap(dx).start()

    for dx in range(4):
        receive_right(dx)
    for dx in range(4):
        swap(dx).wait()

    def pack(block):
        extra = block[16:24]
        top = jnp.where(lane < 96, block[0:8], pltpu.roll(extra, 96, 1))
        middle = jnp.where(lane < 96, block[8:16], pltpu.roll(extra, 64, 1))
        turned = [pltpu.roll(extra, 64, 1), pltpu.roll(extra, 96, 1), extra, pltpu.roll(extra, 32, 1)]
        spread = jnp.zeros((8, 128), F32)
        for q in range(4):
            spread = jnp.where((row % 4 == q) & (lane // 32 == q), turned[q], spread)
        first = jnp.sum(spread[0:4], axis=0, keepdims=True)
        second = jnp.sum(spread[4:8], axis=0, keepdims=True)
        low = jnp.where(row == 0, first, second)
        return jnp.concatenate([top, middle, low, low], axis=0).astype(BF16)

    def multiply(at, pair):
        arrived = left_in.at[pl.ds(0, 31 if pair[0] == 0 else 32), used]
        pltpu.make_async_copy(arrived, arrived, s_left_in.at[at]).wait()
        places = [(z + 8 - dz) % 8 for dz in pair]

        def assemble(dx, _):
            first = ((x + 4 - dx) % 4) * 32
            for h, pz in enumerate(places):
                for q in range(2):
                    left0 = unpack(left_in, first + 16 * q + pz, False)
                    left1 = unpack(left_in, first + 16 * q + 8 + pz, False)
                    columns = pl.ds(pl.multiple_of(256 * dx + 128 * q, 128), 128)
                    a_ref[48 * h : 48 * h + 48, columns] = jnp.concatenate(left0 + left1, axis=0).astype(BF16)
            return 0

        lax.fori_loop(0, 4, assemble, 0)

        def step(px, _):
            product = dot(a_ref[...], b_ref[pl.ds(2 * px, 2)].reshape(256, 1024), 1, 1)
            for h, pz in enumerate(places):
                for q in range(2):
                    for g in range(2):
                        block = product[48 * h + 24 * g : 48 * h + 24 * g + 24, 128 * q : 128 * q + 128]
                        back_ref[px * 32 + 16 * q + 8 * g + pz] = pack(block)
            return 0

        lax.fori_loop(0, 4, step, 0)
        send_pair(back_ref, home_ref, s_back, s_home.at[at], pair, -1)

    for at, pair in enumerate(PAIRS):
        multiply(at, pair)
    home_ref[me] = back_ref[me]
    others = pl.ds(0, CHIPS - 1)
    pltpu.make_async_copy(left_out.at[others, used], left_out.at[others, used], s_left_out).wait()
    pltpu.make_async_copy(right_out.at[others, used], right_out.at[others, used], s_right_out).wait()

    def widen(c, _):
        sums_ref[pl.ds(pl.multiple_of(c * ROWS, 8), ROWS), :] = home_ref[c].astype(F32)[0:ROWS]
        return 0

    for at, pair in enumerate(PAIRS):
        arrived = home_ref.at[pl.ds(0, 31 if pair[0] == 0 else 32), used]
        pltpu.make_async_copy(arrived, arrived, s_home.at[at]).wait()
        for dz in pair:
            pz = (z + dz) % 8
            lax.fori_loop(0, 16, lambda r, _, pz=pz: widen(8 * r + pz, _), 0, unroll=4)

    lanes = lax.broadcasted_iota(jnp.int32, (CHIPS, 128), 1)

    def rows_at(at):
        return sums_ref[pl.ds(at, CHIPS, stride=ROWS), :]

    def finish_main(i, _):
        finish(i, rows_at(i))
        return 0

    def finish_rest(r, q):
        low = rows_at(16 + r // 4)
        shift = (64 - 32 * q) % 128
        low = pltpu.roll(low, shift, 1) if shift else low
        high = jnp.where(lanes < 32, pltpu.roll(rows_at(r), 32, 1), pltpu.roll(rows_at(8 + r), 64, 1))
        finish(16 + r, jnp.where(lanes < 64, high, low))

    def finish(i, values):
        mean = jnp.mean(values, axis=0, keepdims=True)
        centred = values - mean
        spread = jnp.mean(centred * centred, axis=0, keepdims=True)
        normed = (centred * lax.rsqrt(spread + EPS) * gain_ref[...] + bias_ref[...]).astype(BF16)
        projected = dot(normed, w_out_ref[...], 0, 0)
        natural = jnp.concatenate([projected[0:24], projected[48:72], projected[24:48], projected[72:96]], axis=0)
        out_ref[i] = (gate_ref[i] * natural).astype(BF16)

    lax.fori_loop(0, 16, finish_main, 0, unroll=4)

    def finish_four(h, _):
        for q in range(4):
            finish_rest(4 * h + q, q)
        return 0

    lax.fori_loop(0, 2, finish_four, 0)
    pltpu.make_async_copy(back_ref.at[others, used], back_ref.at[others, used], s_back).wait()


def shards(pair, tile_mask, chain_ids, in_gain, in_bias, w_ab, w_gate, out_gain, out_bias, w_out):
    args = (
        pair, tile_mask, chain_ids.reshape(6, 128), in_gain.reshape(1, C), in_bias.reshape(1, C), w_ab, w_gate,
        out_gain.reshape(1, C), out_bias.reshape(1, C), w_out,
    )
    args = tuple(pltpu.with_memory_space_constraint(arg, pltpu.HBM) for arg in args)
    return pl.pallas_call(
        kernel,
        out_shape=pltpu.VMEM((ROWS, COLS, C), BF16),
        in_specs=[pl.BlockSpec(memory_space=pltpu.HBM)] * len(args),
        out_specs=pl.BlockSpec(memory_space=pltpu.VMEM),
        scratch_shapes=[pltpu.VMEM(arg.shape, arg.dtype) for arg in args]
        + [
            pltpu.VMEM((ROWS, COLS, C), BF16),
            pltpu.VMEM((TILES, 128, C), BF16),
            pltpu.VMEM((TILES, 128), F32),
            pltpu.VMEM((512, C), BF16),
            pltpu.VMEM((32 * STAGE, 128), F32),
            pltpu.VMEM((CHIPS, SLOT, 128), BF16),
            pltpu.VMEM((CHIPS, SLOT, 128), BF16),
            pltpu.VMEM((CHIPS, SLOT, 128), BF16),
            pltpu.VMEM((CHIPS, SLOT, 128), BF16),
            pltpu.VMEM((ROWS, COLS, C), F32),
            pltpu.VMEM((96, 1024), BF16),
            pltpu.VMEM((8, 128, 1024), BF16),
            pltpu.VMEM((CHIPS, SLOT, 128), BF16),
            pltpu.VMEM((CHIPS, SLOT, 128), BF16),
            pltpu.VMEM((CHIPS * ROWS, 128), F32),
            pltpu.VMEM((C, 128), F32),
            pltpu.VMEM((C, 128), F32),
            pltpu.SemaphoreType.DMA((len(args),)),
            pltpu.SemaphoreType.REGULAR,
            pltpu.SemaphoreType.REGULAR,
            pltpu.SemaphoreType.DMA(()),
            pltpu.SemaphoreType.DMA(()),
            pltpu.SemaphoreType.DMA((4,)),
            pltpu.SemaphoreType.DMA((4,)),
            pltpu.SemaphoreType.DMA((4,)),
            pltpu.SemaphoreType.DMA((4,)),
            pltpu.SemaphoreType.DMA(()),
            pltpu.SemaphoreType.DMA((4,)),
        ],
        compiler_params=pltpu.CompilerParams(collective_id=1, has_side_effects=True, vmem_limit_bytes=40 << 20),
    )(*args)


def solution(mesh):
    in_specs = (P("wide", "narrow", None), P(), P(), P(), P(), P(), P(), P(), P(), P())
    out_specs = P("wide", "narrow", None)
    return jax.shard_map(shards, mesh=mesh, in_specs=in_specs, out_specs=out_specs, check_vma=False)
```

```python
import functools

import jax
import jax.numpy as jnp
from jax import lax
from jax.experimental import pallas as pl
from jax.experimental.pallas import tpu as pltpu
from jax.sharding import PartitionSpec as P

MESH = pl.DeviceIdType.MESH
F32, BF16 = jnp.float32, jnp.bfloat16
CHIPS = 128
ROWS, COLS, C = 24, 96, 128
MSG, SLOT, STAGE = 18, 32, 48
TILES = 18
PAIRS = ((3, 5), (0, 4), (2, 6), (1, 7))
EPS = 1e-05


def sigmoid(x):
    return 0.5 * jnp.tanh(0.5 * x) + 0.5


def dot(a, b, ca, cb):
    return lax.dot_general(a, b, (((ca,), (cb,)), ((), ())), preferred_element_type=F32)


def keep_mask(wide, narrow, tile_ref, chain_ref):
    tile = lax.broadcasted_iota(jnp.int32, (TILES, 128), 0)
    lane = lax.broadcasted_iota(jnp.int32, (TILES, 128), 1)
    body, main = tile < 16, lane < 96
    i = jnp.where(body, jnp.where(main, tile, 16 + tile % 8), 16 + 4 * (tile - 16) + lane // 32)
    k = jnp.where(body, jnp.where(main, lane, lane - 96 + 32 * (tile // 8)), 64 + lane % 32)
    i = i + wide * ROWS
    k = k + narrow * COLS
    chain_i = jnp.zeros((TILES, 128), jnp.int32)
    chain_k = jnp.zeros((TILES, 128), jnp.int32)
    chains = chain_ref[...]
    for q in range(1, 4):
        below = (chains < q).astype(F32)
        start = jnp.sum(jnp.sum(below, axis=0, keepdims=True), axis=1, keepdims=True).astype(jnp.int32)
        chain_i = chain_i + (i >= start).astype(jnp.int32)
        chain_k = chain_k + (k >= start).astype(jnp.int32)
    same = (chain_i == chain_k).astype(F32)
    row_tile, col_tile = i // 128, k // 128
    blocked = jnp.zeros((TILES, 128), F32)
    for a in range(6):
        in_row = row_tile == a
        for b in range(6):
            value = tile_ref[a : a + 1, b : b + 1].astype(F32)
            blocked = blocked + jnp.where(in_row & (col_tile == b), value, 0.0)
    return jnp.maximum(blocked, same)


def kernel(
    pair_hbm, tile_hbm, chain_hbm, in_gain_hbm, in_bias_hbm, w_ab_hbm, w_gate_hbm, out_gain_hbm, out_bias_hbm, w_out_hbm,
    out_ref,
    pair_ref, tile_ref, chain_ref, in_gain_ref, in_bias_ref, w_ab_ref, w_gate_ref, out_gain_ref, out_bias_ref, w_out_ref,
    normed_ref, packed_ref, mask_ref, w_t_ref, stage_ref, left_out, right_out, left_in, right_in, gate_ref, a_ref, b_ref,
    back_ref, home_ref, sums_ref, gain_ref, bias_ref,
    s_in, s_line, s_plane, s_left_out, s_right_out, s_left_in, s_right_in, s_swap_send, s_swap_recv, s_back, s_home,
):
    wide, narrow = lax.axis_index("wide"), lax.axis_index("narrow")
    w16, core = wide // 2, wide % 2
    y_lo, z = wide // 16, w16 % 8
    x, y = narrow // 2, (narrow % 2) * 2 + y_lo
    me = x * 32 + y * 8 + z

    def device_at(px, py, pz):
        return ((py % 2) * 16 + pz * 2 + core, px * 2 + py // 2)

    sibling = (w16 * 2 + 1 - core, narrow)
    line_z = [device_at(x, y, (z + d) % 8) for d in range(1, 8)]
    line_y = [device_at(x, (y + d) % 4, z) for d in range(1, 4)]
    line_x = [device_at((x + d) % 4, y, z) for d in range(1, 4)]

    inputs = [
        pltpu.make_async_copy(source, target, s_in.at[at])
        for at, (source, target) in enumerate((
            (pair_hbm, pair_ref), (tile_hbm, tile_ref), (chain_hbm, chain_ref), (in_gain_hbm, in_gain_ref),
            (in_bias_hbm, in_bias_ref), (w_ab_hbm, w_ab_ref), (w_gate_hbm, w_gate_ref), (out_gain_hbm, out_gain_ref),
            (out_bias_hbm, out_bias_ref), (w_out_hbm, w_out_ref),
        ))
    ]
    for copy in inputs:
        copy.start()

    barrier = pltpu.get_barrier_semaphore()
    greeted = [sibling] + line_z + line_y + line_x
    for device in greeted:
        pl.semaphore_signal(barrier, inc=1, device_id=device, device_id_type=MESH)

    for copy in inputs:
        copy.wait()

    w_t_ref[...] = w_ab_ref[...].T
    mask_ref[...] = keep_mask(wide, narrow, tile_ref, chain_ref)
    ones = jnp.ones((C, 128), BF16)

    def norm_row(i):
        values = pair_ref[i].astype(F32)
        mean = dot(pair_ref[i], ones, 1, 0) * (1.0 / C)
        centred = values - mean
        spread = jnp.mean(centred * centred, axis=1, keepdims=True)
        normed = (centred * lax.rsqrt(spread + EPS) * in_gain_ref[...] + in_bias_ref[...]).astype(BF16)
        normed_ref[i] = normed
        return normed

    def norm_body(i, _):
        packed_ref[i, 0:96] = norm_row(i)
        return 0

    def norm_tail(r, _):
        normed = norm_row(16 + r)
        packed_ref[r, 96:128] = normed[0:32]
        packed_ref[8 + r, 96:128] = normed[32:64]
        packed_ref[16 + r // 4, pl.ds(pl.multiple_of(32 * (r % 4), 32), 32)] = normed[64:96]
        return 0

    lax.fori_loop(0, 16, norm_body, 0, unroll=4)
    lax.fori_loop(0, 8, norm_tail, 0, unroll=4)

    pl.semaphore_wait(barrier, len(greeted))
    for device in line_y:
        pl.semaphore_signal(s_line, inc=1, device_id=device, device_id_type=MESH)

    used = pl.ds(0, MSG)

    def send_chunk(dx):
        px = (x + dx) % 4
        first = pl.multiple_of(px * 32, 32)
        weights = jnp.concatenate([w_t_ref[pl.ds(g * 128 + first, 32), :] for g in range(4)], axis=0)

        def sides(t):
            proj = dot(weights, packed_ref[pl.ds(t, 2)].reshape(256, C), 1, 1)
            result = []
            for q in range(2):
                part = proj[:, 128 * q : 128 * q + 128]
                mask = mask_ref[pl.ds(t + q, 1), :]
                left = mask * sigmoid(part[0:32]) * part[32:64]
                right = mask * sigmoid(part[64:96]) * part[96:128]
                result.append((left, right))
            return result

        def project(h, _):
            t = 2 * h
            for q, (left, right) in enumerate(sides(t)):
                stage_ref[pl.ds(t + q, 32, stride=STAGE), :] = left
                stage_ref[pl.ds(24 + t + q, 32, stride=STAGE), :] = right
            return 0

        lax.fori_loop(0, TILES // 2, project, 0, unroll=3)

        def cast(c):
            start = pl.multiple_of(c * STAGE, 16)
            both = stage_ref[pl.ds(start, STAGE), :]
            left_out[px * 32 + c] = both[0:32].astype(BF16)
            right_out[px * 32 + c] = jnp.concatenate([both[24:48], both[40:48]], axis=0).astype(BF16)

        def send(d, _):
            py, pz = (y + d // 8) % 4, (z + d % 8) % 8
            pltpu.make_async_remote_copy(
                src_ref=right_out.at[px * 32 + py * 8 + pz, used], dst_ref=right_in.at[me, used], send_sem=s_right_out,
                recv_sem=s_right_in.at[dx], device_id=device_at(px, py, pz), device_id_type=MESH,
            ).start()
            return 0

        def cast_body(c, _):
            cast(c)
            return 0

        lax.fori_loop(0, 32, cast_body, 0, unroll=4)
        if dx == 0:
            lax.fori_loop(1, 8, send, 0)
            pl.semaphore_wait(s_line, len(line_y))
            for device in line_x:
                pl.semaphore_signal(s_plane, inc=1, device_id=device, device_id_type=MESH)
            lax.fori_loop(8, 32, send, 0)
        else:
            if dx == 1:
                pl.semaphore_wait(s_plane, len(line_x))
            lax.fori_loop(0, 32, send, 0)

    for dx in range(4):
        send_chunk(dx)

    def send_pair(source, target, s_out, s_in_pair, pair, sign):
        for dz in pair:
            pz = (z + sign * dz + 8) % 8

            def send(r, _, pz=pz):
                px, py = (x + r // 4) % 4, (y + r % 4) % 4
                pltpu.make_async_remote_copy(
                    src_ref=source.at[px * 32 + py * 8 + pz, used], dst_ref=target.at[me, used], send_sem=s_out,
                    recv_sem=s_in_pair, device_id=device_at(px, py, pz), device_id_type=MESH,
                ).start()
                return 0

            lax.fori_loop(1 if dz == 0 else 0, 16, send, 0)

    for at, pair in enumerate(PAIRS):
        send_pair(left_out, left_in, s_left_out, s_left_in.at[at], pair, 1)
    left_in[me] = left_out[me]
    right_in[me] = right_out[me]

    def gates(i, _):
        gate_ref[i] = sigmoid(dot(normed_ref[i], w_gate_ref[...], 1, 0))
        return 0

    lax.fori_loop(0, ROWS, gates, 0, unroll=2)
    gain_ref[...] = jnp.broadcast_to(out_gain_ref[...], (C, 128)).T
    bias_ref[...] = jnp.broadcast_to(out_bias_ref[...], (C, 128)).T
    for p in range(8):
        b_ref[p, 96:128] = jnp.zeros((32, 1024), BF16)

    lane = lax.broadcasted_iota(jnp.int32, (8, 128), 1)
    row = lax.broadcasted_iota(jnp.int32, (8, 128), 0)

    def unpack(ref, slot, last):
        f = ref[slot].astype(F32)
        low = jnp.where(row < 4, f[16:17], f[17:18])
        turned = [pltpu.roll(low, 64, 1), pltpu.roll(low, 32, 1), low, pltpu.roll(low, 96, 1)]
        low = turned[3]
        for q in range(3):
            low = jnp.where(row % 4 == q, turned[q], low)
        rest = jnp.where(lane < 32, pltpu.roll(f[0:8], 32, 1), jnp.where(lane < 64, pltpu.roll(f[8:16], 64, 1), low))
        if last:
            return [f[0:8], f[8:16], rest]
        zero = jnp.zeros((8, 128), F32)
        return [jnp.where(lane < 96, part, zero) for part in (f[0:8], f[8:16], rest)]

    mine = pl.ds(pl.multiple_of(core * 48, 16), 48)

    def swap(dx):
        half = b_ref.at[:, mine, 256 * dx : 256 * dx + 256]
        return pltpu.make_async_remote_copy(
            src_ref=half, dst_ref=half, send_sem=s_swap_send.at[dx], recv_sem=s_swap_recv.at[dx], device_id=sibling,
            device_id_type=MESH,
        )

    def receive_right(dx):
        arrived = right_in.at[pl.ds(0, 31 if dx == 0 else 32), used]
        pltpu.make_async_copy(arrived, arrived, s_right_in.at[dx]).wait()
        first = ((x + 4 - dx) % 4) * 32

        def assemble(p, _):
            for q in range(2):
                right0 = unpack(right_in, first + 16 * q + 2 * p, True)
                right1 = unpack(right_in, first + 16 * q + 2 * p + 1, True)
                columns = slice(256 * dx + 128 * q, 256 * dx + 128 * q + 128)
                b_ref[p, mine, columns] = jnp.concatenate(right0 + right1, axis=0).astype(BF16)
            return 0

        lax.fori_loop(0, 8, assemble, 0)
        swap(dx).start()

    for dx in range(4):
        receive_right(dx)
    for dx in range(4):
        swap(dx).wait()

    def pack(block):
        extra = block[16:24]
        top = jnp.where(lane < 96, block[0:8], pltpu.roll(extra, 96, 1))
        middle = jnp.where(lane < 96, block[8:16], pltpu.roll(extra, 64, 1))
        turned = [pltpu.roll(extra, 64, 1), pltpu.roll(extra, 96, 1), extra, pltpu.roll(extra, 32, 1)]
        spread = jnp.zeros((8, 128), F32)
        for q in range(4):
            spread = jnp.where((row % 4 == q) & (lane // 32 == q), turned[q], spread)
        first = jnp.sum(spread[0:4], axis=0, keepdims=True)
        second = jnp.sum(spread[4:8], axis=0, keepdims=True)
        low = jnp.where(row == 0, first, second)
        return jnp.concatenate([top, middle, low, low], axis=0).astype(BF16)

    def multiply(at, pair):
        arrived = left_in.at[pl.ds(0, 31 if pair[0] == 0 else 32), used]
        pltpu.make_async_copy(arrived, arrived, s_left_in.at[at]).wait()
        places = [(z + 8 - dz) % 8 for dz in pair]

        def assemble(dx, _):
            first = ((x + 4 - dx) % 4) * 32
            for h, pz in enumerate(places):
                for q in range(2):
                    left0 = unpack(left_in, first + 16 * q + pz, False)
                    left1 = unpack(left_in, first + 16 * q + 8 + pz, False)
                    columns = pl.ds(pl.multiple_of(256 * dx + 128 * q, 128), 128)
                    a_ref[48 * h : 48 * h + 48, columns] = jnp.concatenate(left0 + left1, axis=0).astype(BF16)
            return 0

        lax.fori_loop(0, 4, assemble, 0)

        def step(px, _):
            product = dot(a_ref[...], b_ref[pl.ds(2 * px, 2)].reshape(256, 1024), 1, 1)
            for h, pz in enumerate(places):
                for q in range(2):
                    for g in range(2):
                        block = product[48 * h + 24 * g : 48 * h + 24 * g + 24, 128 * q : 128 * q + 128]
                        back_ref[px * 32 + 16 * q + 8 * g + pz] = pack(block)
            return 0

        lax.fori_loop(0, 4, step, 0)
        send_pair(back_ref, home_ref, s_back, s_home.at[at], pair, -1)

    for at, pair in enumerate(PAIRS):
        multiply(at, pair)
    home_ref[me] = back_ref[me]
    others = pl.ds(0, CHIPS - 1)
    pltpu.make_async_copy(left_out.at[others, used], left_out.at[others, used], s_left_out).wait()
    pltpu.make_async_copy(right_out.at[others, used], right_out.at[others, used], s_right_out).wait()

    def widen(c, _):
        sums_ref[pl.ds(pl.multiple_of(c * ROWS, 8), ROWS), :] = home_ref[c].astype(F32)[0:ROWS]
        return 0

    for at, pair in enumerate(PAIRS):
        arrived = home_ref.at[pl.ds(0, 31 if pair[0] == 0 else 32), used]
        pltpu.make_async_copy(arrived, arrived, s_home.at[at]).wait()
        for dz in pair:
            pz = (z + dz) % 8
            lax.fori_loop(0, 16, lambda r, _, pz=pz: widen(8 * r + pz, _), 0, unroll=16)

    lanes = lax.broadcasted_iota(jnp.int32, (CHIPS, 128), 1)

    def rows_at(at):
        return sums_ref[pl.ds(at, CHIPS, stride=ROWS), :]

    def finish_main(i, _):
        finish(i, rows_at(i))
        return 0

    def finish_rest(r, q):
        low = rows_at(16 + r // 4)
        shift = (64 - 32 * q) % 128
        low = pltpu.roll(low, shift, 1) if shift else low
        high = jnp.where(lanes < 32, pltpu.roll(rows_at(r), 32, 1), pltpu.roll(rows_at(8 + r), 64, 1))
        finish(16 + r, jnp.where(lanes < 64, high, low))

    def finish(i, values):
        mean = jnp.mean(values, axis=0, keepdims=True)
        centred = values - mean
        spread = jnp.mean(centred * centred, axis=0, keepdims=True)
        normed = (centred * lax.rsqrt(spread + EPS) * gain_ref[...] + bias_ref[...]).astype(BF16)
        projected = dot(normed, w_out_ref[...], 0, 0)
        natural = jnp.concatenate([projected[0:24], projected[48:72], projected[24:48], projected[72:96]], axis=0)
        out_ref[i] = (gate_ref[i] * natural).astype(BF16)

    lax.fori_loop(0, 16, finish_main, 0, unroll=8)

    def finish_four(h, _):
        for q in range(4):
            finish_rest(4 * h + q, q)
        return 0

    lax.fori_loop(0, 2, finish_four, 0, unroll=2)
    pltpu.make_async_copy(back_ref.at[others, used], back_ref.at[others, used], s_back).wait()


def shards(pair, tile_mask, chain_ids, in_gain, in_bias, w_ab, w_gate, out_gain, out_bias, w_out):
    args = (
        pair, tile_mask, chain_ids.reshape(6, 128), in_gain.reshape(1, C), in_bias.reshape(1, C), w_ab, w_gate,
        out_gain.reshape(1, C), out_bias.reshape(1, C), w_out,
    )
    args = tuple(pltpu.with_memory_space_constraint(arg, pltpu.HBM) for arg in args)
    return pl.pallas_call(
        kernel,
        out_shape=pltpu.VMEM((ROWS, COLS, C), BF16),
        in_specs=[pl.BlockSpec(memory_space=pltpu.HBM)] * len(args),
        out_specs=pl.BlockSpec(memory_space=pltpu.VMEM),
        scratch_shapes=[pltpu.VMEM(arg.shape, arg.dtype) for arg in args]
        + [
            pltpu.VMEM((ROWS, COLS, C), BF16),
            pltpu.VMEM((TILES, 128, C), BF16),
            pltpu.VMEM((TILES, 128), F32),
            pltpu.VMEM((512, C), BF16),
            pltpu.VMEM((32 * STAGE, 128), F32),
            pltpu.VMEM((CHIPS, SLOT, 128), BF16),
            pltpu.VMEM((CHIPS, SLOT, 128), BF16),
            pltpu.VMEM((CHIPS, SLOT, 128), BF16),
            pltpu.VMEM((CHIPS, SLOT, 128), BF16),
            pltpu.VMEM((ROWS, COLS, C), F32),
            pltpu.VMEM((96, 1024), BF16),
            pltpu.VMEM((8, 128, 1024), BF16),
            pltpu.VMEM((CHIPS, SLOT, 128), BF16),
            pltpu.VMEM((CHIPS, SLOT, 128), BF16),
            pltpu.VMEM((CHIPS * ROWS, 128), F32),
            pltpu.VMEM((C, 128), F32),
            pltpu.VMEM((C, 128), F32),
            pltpu.SemaphoreType.DMA((len(args),)),
            pltpu.SemaphoreType.REGULAR,
            pltpu.SemaphoreType.REGULAR,
            pltpu.SemaphoreType.DMA(()),
            pltpu.SemaphoreType.DMA(()),
            pltpu.SemaphoreType.DMA((4,)),
            pltpu.SemaphoreType.DMA((4,)),
            pltpu.SemaphoreType.DMA((4,)),
            pltpu.SemaphoreType.DMA((4,)),
            pltpu.SemaphoreType.DMA(()),
            pltpu.SemaphoreType.DMA((4,)),
        ],
        compiler_params=pltpu.CompilerParams(collective_id=1, has_side_effects=True, vmem_limit_bytes=40 << 20),
    )(*args)


def solution(mesh):
    in_specs = (P("wide", "narrow", None), P(), P(), P(), P(), P(), P(), P(), P(), P())
    out_specs = P("wide", "narrow", None)
    return jax.shard_map(shards, mesh=mesh, in_specs=in_specs, out_specs=out_specs, check_vma=False)
```

```python
import functools

import jax
import jax.numpy as jnp
from jax import lax
from jax.experimental import pallas as pl
from jax.experimental.pallas import tpu as pltpu
from jax.sharding import PartitionSpec as P

MESH = pl.DeviceIdType.MESH
F32, BF16 = jnp.float32, jnp.bfloat16
CHIPS = 128
ROWS, COLS, C = 24, 96, 128
MSG, SLOT, STAGE = 18, 32, 48
TILES = 18
PAIRS = ((3, 5), (0, 4), (2, 6), (1, 7))
EPS = 1e-05


def sigmoid(x):
    return 0.5 * jnp.tanh(0.5 * x) + 0.5


def dot(a, b, ca, cb):
    return lax.dot_general(a, b, (((ca,), (cb,)), ((), ())), preferred_element_type=F32)


def keep_mask(wide, narrow, tile_ref, chain_ref):
    tile = lax.broadcasted_iota(jnp.int32, (TILES, 128), 0)
    lane = lax.broadcasted_iota(jnp.int32, (TILES, 128), 1)
    body, main = tile < 16, lane < 96
    i = jnp.where(body, jnp.where(main, tile, 16 + tile % 8), 16 + 4 * (tile - 16) + lane // 32)
    k = jnp.where(body, jnp.where(main, lane, lane - 96 + 32 * (tile // 8)), 64 + lane % 32)
    i = i + wide * ROWS
    k = k + narrow * COLS
    chain_i = jnp.zeros((TILES, 128), jnp.int32)
    chain_k = jnp.zeros((TILES, 128), jnp.int32)
    chains = chain_ref[...]
    for q in range(1, 4):
        below = (chains < q).astype(F32)
        start = jnp.sum(jnp.sum(below, axis=0, keepdims=True), axis=1, keepdims=True).astype(jnp.int32)
        chain_i = chain_i + (i >= start).astype(jnp.int32)
        chain_k = chain_k + (k >= start).astype(jnp.int32)
    same = (chain_i == chain_k).astype(F32)
    row_tile, col_tile = i // 128, k // 128
    blocked = jnp.zeros((TILES, 128), F32)
    for a in range(6):
        in_row = row_tile == a
        for b in range(6):
            value = tile_ref[a : a + 1, b : b + 1].astype(F32)
            blocked = blocked + jnp.where(in_row & (col_tile == b), value, 0.0)
    return jnp.maximum(blocked, same)


def kernel(
    pair_hbm, tile_hbm, chain_hbm, in_gain_hbm, in_bias_hbm, w_ab_hbm, w_gate_hbm, out_gain_hbm, out_bias_hbm, w_out_hbm,
    out_ref,
    pair_ref, tile_ref, chain_ref, in_gain_ref, in_bias_ref, w_ab_ref, w_gate_ref, out_gain_ref, out_bias_ref, w_out_ref,
    normed_ref, packed_ref, mask_ref, w_t_ref, stage_ref, left_out, right_out, left_in, right_in, gate_ref, a_ref, b_ref,
    back_ref, home_ref, sums_ref, gain_ref, bias_ref,
    s_in, s_line, s_plane, s_left_out, s_right_out, s_left_in, s_right_in, s_swap_send, s_swap_recv, s_back, s_home,
):
    wide, narrow = lax.axis_index("wide"), lax.axis_index("narrow")
    w16, core = wide // 2, wide % 2
    y_lo, z = wide // 16, w16 % 8
    x, y = narrow // 2, (narrow % 2) * 2 + y_lo
    me = x * 32 + y * 8 + z

    def device_at(px, py, pz):
        return ((py % 2) * 16 + pz * 2 + core, px * 2 + py // 2)

    sibling = (w16 * 2 + 1 - core, narrow)
    line_z = [device_at(x, y, (z + d) % 8) for d in range(1, 8)]
    line_y = [device_at(x, (y + d) % 4, z) for d in range(1, 4)]
    line_x = [device_at((x + d) % 4, y, z) for d in range(1, 4)]

    inputs = [
        pltpu.make_async_copy(source, target, s_in.at[at])
        for at, (source, target) in enumerate((
            (pair_hbm, pair_ref), (tile_hbm, tile_ref), (chain_hbm, chain_ref), (in_gain_hbm, in_gain_ref),
            (in_bias_hbm, in_bias_ref), (w_ab_hbm, w_ab_ref), (w_gate_hbm, w_gate_ref), (out_gain_hbm, out_gain_ref),
            (out_bias_hbm, out_bias_ref), (w_out_hbm, w_out_ref),
        ))
    ]
    for copy in inputs:
        copy.start()

    barrier = pltpu.get_barrier_semaphore()
    greeted = [sibling] + line_z + line_y + line_x
    for device in greeted:
        pl.semaphore_signal(barrier, inc=1, device_id=device, device_id_type=MESH)

    for copy in inputs:
        copy.wait()

    w_t_ref[...] = w_ab_ref[...].T
    mask_ref[...] = keep_mask(wide, narrow, tile_ref, chain_ref)
    ones = jnp.ones((C, 128), BF16)

    def norm_row(i):
        values = pair_ref[i].astype(F32)
        mean = dot(pair_ref[i], ones, 1, 0) * (1.0 / C)
        centred = values - mean
        spread = jnp.mean(centred * centred, axis=1, keepdims=True)
        normed = (centred * lax.rsqrt(spread + EPS) * in_gain_ref[...] + in_bias_ref[...]).astype(BF16)
        normed_ref[i] = normed
        return normed

    def norm_body(i, _):
        packed_ref[i, 0:96] = norm_row(i)
        return 0

    def norm_tail(r, _):
        normed = norm_row(16 + r)
        packed_ref[r, 96:128] = normed[0:32]
        packed_ref[8 + r, 96:128] = normed[32:64]
        packed_ref[16 + r // 4, pl.ds(pl.multiple_of(32 * (r % 4), 32), 32)] = normed[64:96]
        return 0

    lax.fori_loop(0, 16, norm_body, 0, unroll=4)
    lax.fori_loop(0, 8, norm_tail, 0, unroll=4)

    pl.semaphore_wait(barrier, len(greeted))
    for device in line_y:
        pl.semaphore_signal(s_line, inc=1, device_id=device, device_id_type=MESH)

    used = pl.ds(0, MSG)

    def send_chunk(dx):
        px = (x + dx) % 4
        first = pl.multiple_of(px * 32, 32)
        weights = jnp.concatenate([w_t_ref[pl.ds(g * 128 + first, 32), :] for g in range(4)], axis=0)

        def sides(t):
            proj = dot(weights, packed_ref[pl.ds(t, 2)].reshape(256, C), 1, 1)
            result = []
            for q in range(2):
                part = proj[:, 128 * q : 128 * q + 128]
                mask = mask_ref[pl.ds(t + q, 1), :]
                left = mask * sigmoid(part[0:32]) * part[32:64]
                right = mask * sigmoid(part[64:96]) * part[96:128]
                result.append((left, right))
            return result

        def project(h, _):
            t = 2 * h
            for q, (left, right) in enumerate(sides(t)):
                stage_ref[pl.ds(t + q, 32, stride=STAGE), :] = left
                stage_ref[pl.ds(24 + t + q, 32, stride=STAGE), :] = right
            return 0

        lax.fori_loop(0, TILES // 2, project, 0, unroll=3)

        def cast(c):
            start = pl.multiple_of(c * STAGE, 16)
            both = stage_ref[pl.ds(start, STAGE), :]
            left_out[px * 32 + c] = both[0:32].astype(BF16)
            right_out[px * 32 + c] = jnp.concatenate([both[24:48], both[40:48]], axis=0).astype(BF16)

        def send(d, _):
            py, pz = (y + d // 8) % 4, (z + d % 8) % 8
            pltpu.make_async_remote_copy(
                src_ref=right_out.at[px * 32 + py * 8 + pz, used], dst_ref=right_in.at[me, used], send_sem=s_right_out,
                recv_sem=s_right_in.at[dx], device_id=device_at(px, py, pz), device_id_type=MESH,
            ).start()
            return 0

        def cast_body(c, _):
            cast(c)
            return 0

        lax.fori_loop(0, 32, cast_body, 0, unroll=4)
        if dx == 0:
            lax.fori_loop(1, 8, send, 0)
            pl.semaphore_wait(s_line, len(line_y))
            for device in line_x:
                pl.semaphore_signal(s_plane, inc=1, device_id=device, device_id_type=MESH)
            lax.fori_loop(8, 32, send, 0)
        else:
            if dx == 1:
                pl.semaphore_wait(s_plane, len(line_x))
            lax.fori_loop(0, 32, send, 0)

    for dx in range(4):
        send_chunk(dx)

    def send_pair(source, target, s_out, s_in_pair, pair, sign):
        for dz in pair:
            pz = (z + sign * dz + 8) % 8

            def send(r, _, pz=pz):
                px, py = (x + r // 4) % 4, (y + r % 4) % 4
                pltpu.make_async_remote_copy(
                    src_ref=source.at[px * 32 + py * 8 + pz, used], dst_ref=target.at[me, used], send_sem=s_out,
                    recv_sem=s_in_pair, device_id=device_at(px, py, pz), device_id_type=MESH,
                ).start()
                return 0

            lax.fori_loop(1 if dz == 0 else 0, 16, send, 0)

    for at, pair in enumerate(PAIRS):
        send_pair(left_out, left_in, s_left_out, s_left_in.at[at], pair, 1)
    left_in[me] = left_out[me]
    right_in[me] = right_out[me]

    def gates(i, _):
        gate_ref[i] = sigmoid(dot(normed_ref[i], w_gate_ref[...], 1, 0))
        return 0

    lax.fori_loop(0, ROWS, gates, 0, unroll=2)
    gain_ref[...] = jnp.broadcast_to(out_gain_ref[...], (C, 128)).T
    bias_ref[...] = jnp.broadcast_to(out_bias_ref[...], (C, 128)).T
    for p in range(8):
        b_ref[p, 96:128] = jnp.zeros((32, 1024), BF16)

    lane = lax.broadcasted_iota(jnp.int32, (8, 128), 1)
    row = lax.broadcasted_iota(jnp.int32, (8, 128), 0)

    def unpack(ref, slot, last):
        f = ref[slot].astype(F32)
        low = jnp.where(row < 4, f[16:17], f[17:18])
        turned = [pltpu.roll(low, 64, 1), pltpu.roll(low, 32, 1), low, pltpu.roll(low, 96, 1)]
        low = turned[3]
        for q in range(3):
            low = jnp.where(row % 4 == q, turned[q], low)
        rest = jnp.where(lane < 32, pltpu.roll(f[0:8], 32, 1), jnp.where(lane < 64, pltpu.roll(f[8:16], 64, 1), low))
        if last:
            return [f[0:8], f[8:16], rest]
        zero = jnp.zeros((8, 128), F32)
        return [jnp.where(lane < 96, part, zero) for part in (f[0:8], f[8:16], rest)]

    mine = pl.ds(pl.multiple_of(core * 48, 16), 48)

    def swap(dx):
        half = b_ref.at[:, mine, 256 * dx : 256 * dx + 256]
        return pltpu.make_async_remote_copy(
            src_ref=half, dst_ref=half, send_sem=s_swap_send.at[dx], recv_sem=s_swap_recv.at[dx], device_id=sibling,
            device_id_type=MESH,
        )

    def receive_right(dx):
        arrived = right_in.at[pl.ds(0, 31 if dx == 0 else 32), used]
        pltpu.make_async_copy(arrived, arrived, s_right_in.at[dx]).wait()
        first = ((x + 4 - dx) % 4) * 32

        def assemble(p, _):
            for q in range(2):
                right0 = unpack(right_in, first + 16 * q + 2 * p, True)
                right1 = unpack(right_in, first + 16 * q + 2 * p + 1, True)
                columns = slice(256 * dx + 128 * q, 256 * dx + 128 * q + 128)
                b_ref[p, mine, columns] = jnp.concatenate(right0 + right1, axis=0).astype(BF16)
            return 0

        lax.fori_loop(0, 8, assemble, 0)
        swap(dx).start()

    for dx in range(4):
        receive_right(dx)
    for dx in range(4):
        swap(dx).wait()

    def pack(block):
        extra = block[16:24]
        top = jnp.where(lane < 96, block[0:8], pltpu.roll(extra, 96, 1))
        middle = jnp.where(lane < 96, block[8:16], pltpu.roll(extra, 64, 1))
        turned = [pltpu.roll(extra, 64, 1), pltpu.roll(extra, 96, 1), extra, pltpu.roll(extra, 32, 1)]
        spread = jnp.zeros((8, 128), F32)
        for q in range(4):
            spread = jnp.where((row % 4 == q) & (lane // 32 == q), turned[q], spread)
        first = jnp.sum(spread[0:4], axis=0, keepdims=True)
        second = jnp.sum(spread[4:8], axis=0, keepdims=True)
        low = jnp.where(row == 0, first, second)
        return jnp.concatenate([top, middle, low, low], axis=0).astype(BF16)

    def multiply(at, pair):
        arrived = left_in.at[pl.ds(0, 31 if pair[0] == 0 else 32), used]
        pltpu.make_async_copy(arrived, arrived, s_left_in.at[at]).wait()
        places = [(z + 8 - dz) % 8 for dz in pair]

        def assemble(dx, _):
            first = ((x + 4 - dx) % 4) * 32
            for h, pz in enumerate(places):
                for q in range(2):
                    left0 = unpack(left_in, first + 16 * q + pz, False)
                    left1 = unpack(left_in, first + 16 * q + 8 + pz, False)
                    columns = pl.ds(pl.multiple_of(256 * dx + 128 * q, 128), 128)
                    a_ref[48 * h : 48 * h + 48, columns] = jnp.concatenate(left0 + left1, axis=0).astype(BF16)
            return 0

        lax.fori_loop(0, 4, assemble, 0)

        def step(px, _):
            product = dot(a_ref[...], b_ref[pl.ds(2 * px, 2)].reshape(256, 1024), 1, 1)
            for h, pz in enumerate(places):
                for q in range(2):
                    for g in range(2):
                        block = product[48 * h + 24 * g : 48 * h + 24 * g + 24, 128 * q : 128 * q + 128]
                        back_ref[px * 32 + 16 * q + 8 * g + pz] = pack(block)
            return 0

        lax.fori_loop(0, 4, step, 0)
        send_pair(back_ref, home_ref, s_back, s_home.at[at], pair, -1)

    for at, pair in enumerate(PAIRS):
        multiply(at, pair)
    home_ref[me] = back_ref[me]
    others = pl.ds(0, CHIPS - 1)
    pltpu.make_async_copy(left_out.at[others, used], left_out.at[others, used], s_left_out).wait()
    pltpu.make_async_copy(right_out.at[others, used], right_out.at[others, used], s_right_out).wait()

    def widen(c, _):
        sums_ref[pl.ds(pl.multiple_of(c * ROWS, 8), ROWS), :] = home_ref[c].astype(F32)[0:ROWS]
        return 0

    for at, pair in enumerate(PAIRS):
        arrived = home_ref.at[pl.ds(0, 31 if pair[0] == 0 else 32), used]
        pltpu.make_async_copy(arrived, arrived, s_home.at[at]).wait()
        for dz in pair:
            pz = (z + dz) % 8
            lax.fori_loop(0, 16, lambda r, _, pz=pz: widen(8 * r + pz, _), 0, unroll=16)

    lanes = lax.broadcasted_iota(jnp.int32, (CHIPS, 128), 1)

    def rows_at(at):
        return sums_ref[pl.ds(at, CHIPS, stride=ROWS), :]

    def finish_main(i, _):
        finish(i, rows_at(i))
        return 0

    def finish_rest(r, q):
        low = rows_at(16 + r // 4)
        shift = (64 - 32 * q) % 128
        low = pltpu.roll(low, shift, 1) if shift else low
        high = jnp.where(lanes < 32, pltpu.roll(rows_at(r), 32, 1), pltpu.roll(rows_at(8 + r), 64, 1))
        finish(16 + r, jnp.where(lanes < 64, high, low))

    def finish(i, values):
        mean = jnp.mean(values, axis=0, keepdims=True)
        centred = values - mean
        spread = jnp.mean(centred * centred, axis=0, keepdims=True)
        normed = (centred * lax.rsqrt(spread + EPS) * gain_ref[...] + bias_ref[...]).astype(BF16)
        projected = dot(normed, w_out_ref[...], 0, 0)
        natural = jnp.concatenate([projected[0:24], projected[48:72], projected[24:48], projected[72:96]], axis=0)
        out_ref[i] = (gate_ref[i] * natural).astype(BF16)

    lax.fori_loop(0, 16, finish_main, 0, unroll=8)

    def finish_four(h, _):
        for q in range(4):
            finish_rest(4 * h + q, q)
        return 0

    lax.fori_loop(0, 2, finish_four, 0, unroll=2)
    pltpu.make_async_copy(back_ref.at[others, used], back_ref.at[others, used], s_back).wait()


def shards(pair, tile_mask, chain_ids, in_gain, in_bias, w_ab, w_gate, out_gain, out_bias, w_out):
    args = (
        pair, tile_mask, chain_ids.reshape(6, 128), in_gain.reshape(1, C), in_bias.reshape(1, C), w_ab, w_gate,
        out_gain.reshape(1, C), out_bias.reshape(1, C), w_out,
    )
    args = tuple(pltpu.with_memory_space_constraint(arg, pltpu.HBM) for arg in args)
    return pl.pallas_call(
        kernel,
        out_shape=pltpu.VMEM((ROWS, COLS, C), BF16),
        in_specs=[pl.BlockSpec(memory_space=pltpu.HBM)] * len(args),
        out_specs=pl.BlockSpec(memory_space=pltpu.VMEM),
        scratch_shapes=[pltpu.VMEM(arg.shape, arg.dtype) for arg in args]
        + [
            pltpu.VMEM((ROWS, COLS, C), BF16),
            pltpu.VMEM((TILES, 128, C), BF16),
            pltpu.VMEM((TILES, 128), F32),
            pltpu.VMEM((512, C), BF16),
            pltpu.VMEM((33 * STAGE, 128), F32),
            pltpu.VMEM((CHIPS, SLOT, 128), BF16),
            pltpu.VMEM((CHIPS, SLOT, 128), BF16),
            pltpu.VMEM((CHIPS, SLOT, 128), BF16),
            pltpu.VMEM((CHIPS, SLOT, 128), BF16),
            pltpu.VMEM((ROWS, COLS, C), F32),
            pltpu.VMEM((96, 1024), BF16),
            pltpu.VMEM((8, 128, 1024), BF16),
            pltpu.VMEM((CHIPS, SLOT, 128), BF16),
            pltpu.VMEM((CHIPS, SLOT, 128), BF16),
            pltpu.VMEM(((CHIPS + 1) * ROWS, 128), F32),
            pltpu.VMEM((C, 128), F32),
            pltpu.VMEM((C, 128), F32),
            pltpu.SemaphoreType.DMA((len(args),)),
            pltpu.SemaphoreType.REGULAR,
            pltpu.SemaphoreType.REGULAR,
            pltpu.SemaphoreType.DMA(()),
            pltpu.SemaphoreType.DMA(()),
            pltpu.SemaphoreType.DMA((4,)),
            pltpu.SemaphoreType.DMA((4,)),
            pltpu.SemaphoreType.DMA((4,)),
            pltpu.SemaphoreType.DMA((4,)),
            pltpu.SemaphoreType.DMA(()),
            pltpu.SemaphoreType.DMA((4,)),
        ],
        compiler_params=pltpu.CompilerParams(collective_id=1, has_side_effects=True, vmem_limit_bytes=40 << 20),
    )(*args)


def solution(mesh):
    in_specs = (P("wide", "narrow", None), P(), P(), P(), P(), P(), P(), P(), P(), P())
    out_specs = P("wide", "narrow", None)
    return jax.shard_map(shards, mesh=mesh, in_specs=in_specs, out_specs=out_specs, check_vma=False)
```
